32 devices in a mesh: seq: 8 (over z, x), tp: 4 (over y, core).
Axes of the slice: x: 2, y: 2, z: 4, core: 2. Of those that a mesh axis runs over, the one named last changes fastest.
Arguments:
- queries: bfloat16 [2048, 1024], P('seq', 'tp'), may hold values from -6 to 6
- keys: bfloat16 [2048, 1024], P('seq', 'tp'), may hold values from -6 to 6
- values: bfloat16 [2048, 1024], P('seq', 'tp'), may hold values from -6 to 6
- out_weight: bfloat16 [1024, 5120], P('tp'), may hold values from -0.375 to 0.375
- residual: bfloat16 [2048, 5120], P(('seq', 'tp')), may hold values from -3 to 3
- gate: float32 [5120], replicated, may hold values from 0.5 to 1.5
- block_mask: int32 [16, 16], replicated, may hold values from 0 to 1, as said below
Outputs:
- updated: bfloat16 [2048, 5120], P(('seq', 'tp'))
The draws below stay inside these ranges and needn't reach their ends.
Inputs may be any that keep to these rules, and one draw needn't show every extreme that they name: block_mask[i, j] is 1 wherever |i - j| <= 4. Group the blocks by index of seq, 2 consecutive blocks to an index; where two indices lie more than 2 apart, the rows of one index's query blocks name at most one key block of the other index, and for indices exactly 3 apart this most is always reached.
All inputs are finite; a program needn't handle non-finite values.
Results may differ from the reference program's by a relative error of at most 0.012.
Values may be sent and summed in bfloat16 or wider, within the bound.
No kernel may reach another device: no remote copies, remote signals or barrier semaphores. Data moves between devices by JAX's collectives and lax.ppermute only.
A program may use at most 128 MiB of HBM per device.

```python
import jax
import jax.numpy as jnp
from jax import lax

D = 5120
HD = 128
HEADS = 8
BLOCK = 128
BLK_DEV = 2
TOKENS = 2048
NB = 16


def paired_draw(key):
    base = jax.random.fold_in(key, 11)
    key_one, key_two = jax.random.split(base, 2)
    width = HEADS * HD
    query_field = 1.4 * jax.random.normal(key_one, (TOKENS, width), jnp.float32)
    key_field = 1.4 * jax.random.normal(key_two, (TOKENS, width), jnp.float32)
    query_field = jnp.clip(query_field, -6.0, 6.0)
    key_field = jnp.clip(key_field, -6.0, 6.0)
    return (query_field, key_field)


def draw_queries(key, part):
    return paired_draw(key)[0].astype(jnp.bfloat16)


def draw_keys(key, part):
    return paired_draw(key)[1].astype(jnp.bfloat16)


def draw_block_mask(key, part):
    per_device = BLK_DEV
    reach = (per_device + 3) // per_device
    device_count = NB // per_device
    rows = jnp.arange(NB, dtype=jnp.int32)[:, None]
    cols = jnp.arange(NB, dtype=jnp.int32)[None, :]
    distance = jnp.abs(rows - cols)
    ticket = jax.random.randint(jax.random.fold_in(key, 5), (NB, NB), 0, 4096)
    lucky = ticket * distance < 16384
    row_device = rows // per_device
    col_device = cols // per_device
    device_gap = jnp.abs(row_device - col_device)
    chosen = jax.random.randint(jax.random.fold_in(key, 7), (device_count, device_count), 0, per_device)
    chosen_here = chosen[row_device, col_device]
    near_keep = (distance <= 4) | lucky
    far_keep = (cols % per_device == chosen_here) & (lucky | (device_gap == reach + 1))
    keep = jnp.where(device_gap <= reach, near_keep, far_keep)
    return keep.astype(jnp.int32)


def levels(key, shape, cuts, low, largest):
    gain = 1.0
    for axis_at, shards_of in cuts:
        heights = jax.random.uniform(jax.random.fold_in(jax.random.fold_in(key, 6), axis_at), (shards_of,), jnp.float32, low / len(cuts), largest / len(cuts))
        gain = gain * jnp.repeat(jnp.exp(heights), shape[axis_at] // shards_of).reshape((-1,) + (1,) * (len(shape) - 1 - axis_at))
    return gain


def bell_draw(key, dims, scale, bound, shards=(), kind=jnp.bfloat16):
    entries = scale * jax.random.normal(key, dims, jnp.float32)
    if shards:
        entries = entries * levels(key, dims, shards, -0.22, 0.18)
    return jnp.clip(entries, -bound, bound).astype(kind)


def setup_inputs(seed: int = 0) -> dict:
    key_of = jax.random.split(jax.random.key(seed), 8)
    return {
        "queries": draw_queries(jax.random.fold_in(key_of[7], 71), 0),
        "keys": draw_keys(jax.random.fold_in(key_of[7], 71), 0),
        "values": bell_draw(key_of[2], (TOKENS, HEADS * HD), 1.0, 6.0, ((0, 8), (1, 4))),
        "out_weight": bell_draw(key_of[3], (HEADS * HD, D), (HD * 2) ** -0.5, 0.375, ((0, 4),)),
        "residual": bell_draw(key_of[4], (TOKENS, D), 0.5, 3.0, ((0, 32),)),
        "gate": jnp.clip(jax.random.uniform(key_of[5], (D,), jnp.float32, 0.5, 1.5), 0.5, 1.5),
        "block_mask": draw_block_mask(jax.random.fold_in(key_of[7], 71), 0),
    }


NEGATIVE = -1.0e30


def reference(queries, keys, values, out_weight, residual, gate, block_mask):
    score_scale = 1.0 / (HD ** 0.5)
    query_blocks = queries.reshape(NB, BLOCK, HEADS, HD)
    key_heads = keys.reshape(TOKENS, HEADS, HD).astype(jnp.float32)
    value_heads = values.reshape(TOKENS, HEADS, HD).astype(jnp.float32)

    def one_block(inputs):
        query_rows, mask_row = inputs
        scores = jnp.einsum("qhd,khd->hqk", query_rows.astype(jnp.float32), key_heads) * score_scale
        allowed = (jnp.repeat(mask_row, BLOCK) > 0)[None, None, :]
        scores = jnp.where(allowed, scores, NEGATIVE)
        row_top = jnp.max(scores, axis=-1, keepdims=True)
        weights = jnp.where(allowed, jnp.exp(scores - row_top), 0.0)
        totals = jnp.sum(weights, axis=-1)
        rounded = weights.astype(jnp.bfloat16).astype(jnp.float32)
        summed = jnp.einsum("hqk,khd->qhd", rounded, value_heads)
        return (summed / jnp.transpose(totals)[:, :, None]).astype(jnp.bfloat16)

    attended = lax.map(one_block, (query_blocks, block_mask)).reshape(TOKENS, HEADS * HD)
    branch = jnp.dot(attended, out_weight, preferred_element_type=jnp.float32)
    return (residual.astype(jnp.float32) + gate[None, :] * branch).astype(jnp.bfloat16)
```

```python
import functools
import math

import jax
import jax.numpy as jnp
from jax import lax
from jax.experimental import pallas as pl
from jax.experimental.pallas import tpu as pltpu
from jax.sharding import PartitionSpec as P

HD = 128
BLOCK = 128
NEGATIVE = -1e30
LOG2E = math.log2(math.e)
SCORE_SCALE = LOG2E / HD**0.5
BATCH = 4

VMEM = pltpu.MemorySpace.VMEM
SMEM = pltpu.MemorySpace.SMEM


def in_vmem(count):
    return [pl.BlockSpec(memory_space=VMEM)] * count


def bf16(*shape):
    return jax.ShapeDtypeStruct(shape, jnp.bfloat16)


def f32(*shape):
    return jax.ShapeDtypeStruct(shape, jnp.float32)


def dot(left, right, contract=((1,), (0,))):
    return lax.dot_general(
        left, right, (contract, ((), ())), preferred_element_type=jnp.float32
    )


def pack(half, q, k, v, kv_keep, kv_send, q_keep, q_send):
    rows, width = q.shape
    part = width // 2
    mine = (lax.axis_index("seq") >= half).astype(jnp.int32)
    keep = pl.ds(pl.multiple_of(mine * part, part), part)
    send = pl.ds(pl.multiple_of((1 - mine) * part, part), part)
    for columns, kv, queries in ((keep, kv_keep, q_keep), (send, kv_send, q_send)):
        kv[:rows] = k[:, columns]
        kv[rows:] = v[:, columns]
        queries[...] = q[:, columns]


def attend(half, cores, places, first, last, *refs):
    mask, q_own, q_far = refs[:3]
    pieces = refs[3 : 3 + len(places)]
    rest = refs[3 + len(places) :]
    if not first:
        old_top, old_total, old_summed = rest[:3]
        rest = rest[3:]
    me = lax.axis_index("seq")
    rows = q_own.shape[0]
    blocks = rows // BLOCK
    heads = q_own.shape[1] // HD
    partner = me ^ half
    query_blocks = [me * blocks + a for a in range(blocks)]
    query_blocks += [partner * blocks + a for a in range(blocks)]
    bias = [
        [
            [
                jnp.where(mask[row, (me ^ place) * blocks + b] > 0, 0.0, NEGATIVE)
                for b in range(blocks)
            ]
            for row in query_blocks
        ]
        for place in places
    ]
    outs = []
    for head in range(heads):
        at = slice(head * HD, (head + 1) * HD)
        queries = jnp.concatenate([q_own[:, at], q_far[:, at]], axis=0)
        scores = []
        for n, piece in enumerate(pieces):
            raw = dot(queries, piece[:rows, at], ((1,), (1,)))
            scores.append(
                [
                    [
                        raw[a * BLOCK : (a + 1) * BLOCK, b * BLOCK : (b + 1) * BLOCK]
                        * SCORE_SCALE
                        + bias[n][a][b]
                        for b in range(blocks)
                    ]
                    for a in range(2 * blocks)
                ]
            )
        for a in range(2 * blocks):
            band = slice(a * BLOCK, (a + 1) * BLOCK)
            tiles = [piece[a][b] for piece in scores for b in range(blocks)]
            high = functools.reduce(jnp.maximum, tiles)
            top = jnp.max(high, axis=1, keepdims=True)
            if not first:
                before = old_top[band, at][:, :1]
                top = jnp.maximum(top, before)
                fade = jnp.exp2(before - top)
            weights = [jnp.exp2(tile - top) for tile in tiles]
            total = functools.reduce(jnp.add, weights)
            summed = None
            for n, piece in enumerate(pieces):
                mine = jnp.concatenate(weights[n * blocks : (n + 1) * blocks], axis=1)
                part = dot(mine.astype(jnp.bfloat16), piece[rows:, at])
                summed = part if summed is None else summed + part
            if not first:
                total = total + old_total[band, at] * fade
                summed = summed + old_summed[band, at] * fade
            if last:
                whole = jnp.sum(total, axis=1, keepdims=True)
                outs.append((summed / whole).astype(jnp.bfloat16))
            else:
                new_top, new_total, new_summed = rest
                new_top[band, at] = jnp.broadcast_to(top, (BLOCK, HD))
                new_total[band, at] = total
                new_summed[band, at] = summed
    if not last:
        return
    own_mine, own_other, far_mine, far_other = rest
    core = lax.rem(lax.axis_index("tp"), cores)
    chips = lax.axis_size("tp") // cores
    share = rows // (chips * cores)
    for head in range(heads):
        at = slice(head * HD, (head + 1) * HD)
        whole = jnp.concatenate(outs[head * 2 * blocks : (head + 1) * 2 * blocks], axis=0)
        for base, mine, other in ((0, own_mine, own_other), (rows, far_mine, far_other)):
            for chip in range(chips):
                start = base + chip * cores * share
                one = whole[start : start + share]
                two = whole[start + share : start + 2 * share]
                to = slice(chip * share, (chip + 1) * share)
                mine[to, at] = jnp.where(core == 0, one, two)
                other[to, at] = jnp.where(core == 0, two, one)


def gather_heads(half, own, far, other, far_other, mine_ref, core_ref):
    low = lax.axis_index("seq") < half
    part = own.shape[1]
    own, far, other, far_other = own[...], far[...], other[...], far_other[...]
    mine_ref[:, :part] = jnp.where(low, own, far)
    mine_ref[:, part:] = jnp.where(low, far, own)
    core_ref[:, :part] = jnp.where(low, other, far_other)
    core_ref[:, part:] = jnp.where(low, far_other, other)


def project_peers(half, cores, own, far, other, far_other, weight, core_weight, *rest):
    outs, (mine, core) = rest[:-2], rest[-2:]
    gather_heads(half, own, far, other, far_other, mine, core)
    chips = lax.axis_size("tp") // cores
    chip = lax.axis_index("tp") // cores
    share = own.shape[0] // chips
    for step, out in enumerate(outs, 1):
        place = lax.rem(chip + step, chips)
        rows = pl.ds(pl.multiple_of(place * share, share), share)
        branch = dot(mine[rows], weight[...]) + dot(core[rows], core_weight[...])
        out[...] = branch.astype(jnp.bfloat16)


def project_own(half, cores, own, far, other, far_other, weight, core_weight, out, mine, core):
    gather_heads(half, own, far, other, far_other, mine, core)
    chips = lax.axis_size("tp") // cores
    chip = lax.axis_index("tp") // cores
    share = own.shape[0] // chips
    rows = pl.ds(pl.multiple_of(chip * share, share), share)
    out[...] = dot(mine[rows], weight[...]) + dot(core[rows], core_weight[...])


def finish(residual, gate, own, *rest):
    peers, out = rest[:-1], rest[-1]
    branch = own[...]
    for peer in peers:
        branch = branch + peer[...].astype(jnp.float32)
    out[...] = (residual[...].astype(jnp.float32) + gate[...] * branch).astype(jnp.bfloat16)


def params(mib):
    return pltpu.CompilerParams(vmem_limit_bytes=mib * 2**20)


def shards(queries, keys, values, out_weight, residual, gate, block_mask):
    rows, width = queries.shape
    columns = out_weight.shape[1]
    seq, tp = lax.axis_size("seq"), lax.axis_size("tp")
    half = seq // 2
    cores = 2
    chips = tp // cores
    share = rows // tp
    part = width // 2

    def swap(array, place):
        return lax.ppermute(array, "seq", [(i, i ^ place) for i in range(seq)])

    def across(array, place, core):
        return lax.ppermute(
            array,
            ("seq", "tp"),
            [
                (i * tp + t, (i ^ place) * tp + (t ^ core))
                for i in range(seq)
                for t in range(tp)
            ],
        )

    kv_keep, kv_send, q_keep, q_send = pl.pallas_call(
        functools.partial(pack, half),
        out_shape=[bf16(2 * rows, part)] * 2 + [bf16(rows, part)] * 2,
        in_specs=in_vmem(3),
        out_specs=in_vmem(4),
        compiler_params=params(16),
        name="pack",
    )(queries, keys, values)
    kv_far = swap(kv_send, half)
    order = list(range(half - 1, 0, -1))
    near = {m: swap(kv_keep, m) for m in order}
    q_far = swap(q_send, half)
    far = {m: swap(kv_far, m) for m in order}
    core_weight = lax.ppermute(out_weight, "tp", [(t, t ^ 1) for t in range(tp)])
    pieces = [(0, kv_keep)] + [(m, near[m]) for m in order]
    pieces += [(half, kv_far)] + [(m ^ half, far[m]) for m in order]
    state = []
    for at in range(0, len(pieces), BATCH):
        batch = pieces[at : at + BATCH]
        first, last = at == 0, at + BATCH >= len(pieces)
        if last:
            out_shape = [bf16(rows // cores, part)] * 4
        else:
            out_shape = [f32(2 * rows, part)] * 3
        state = pl.pallas_call(
            functools.partial(attend, half, cores, [m for m, _ in batch], first, last),
            out_shape=out_shape,
            in_specs=[pl.BlockSpec(memory_space=SMEM)] + in_vmem(2 + len(batch) + len(state)),
            out_specs=in_vmem(len(out_shape)),
            compiler_params=params(32),
            name="attend",
        )(block_mask, q_keep, q_far, *[piece for _, piece in batch], *state)
    own_mine, own_other, far_mine, far_other = state
    from_far = across(far_mine, half, 0)
    from_far_core = across(far_other, half, 1)
    from_core = across(own_other, 0, 1)
    heads = (own_mine, from_far, from_core, from_far_core)
    scratch = [pltpu.VMEM((rows // cores, width), jnp.bfloat16)] * 2
    sums = pl.pallas_call(
        functools.partial(project_peers, half, cores),
        out_shape=[bf16(share, columns)] * (chips - 1),
        in_specs=in_vmem(6),
        out_specs=in_vmem(chips - 1),
        scratch_shapes=scratch,
        compiler_params=params(32),
        name="project_peers",
    )(*heads, out_weight, core_weight)
    arrived = [
        lax.ppermute(
            array,
            "tp",
            [(t, (t // cores + step) % chips * cores + t % cores) for t in range(tp)],
        )
        for step, array in enumerate(sums, 1)
    ]
    own = pl.pallas_call(
        functools.partial(project_own, half, cores),
        out_shape=f32(share, columns),
        in_specs=in_vmem(6),
        out_specs=pl.BlockSpec(memory_space=VMEM),
        scratch_shapes=scratch,
        compiler_params=params(32),
        name="project_own",
    )(*heads, out_weight, core_weight)
    return pl.pallas_call(
        finish,
        out_shape=bf16(share, columns),
        in_specs=in_vmem(3 + len(arrived)),
        out_specs=pl.BlockSpec(memory_space=VMEM),
        compiler_params=params(16),
        name="finish",
    )(residual, gate[None, :], own, *arrived)


def solution(mesh):
    return jax.shard_map(
        shards,
        mesh=mesh,
        in_specs=(
            P("seq", "tp"),
            P("seq", "tp"),
            P("seq", "tp"),
            P("tp", None),
            P(("seq", "tp"), None),
            P(),
            P(),
        ),
        out_specs=P(("seq", "tp"), None),
        check_vma=False,
    )
```

```python
import functools
import math

import jax
import jax.numpy as jnp
from jax import lax
from jax.experimental import pallas as pl
from jax.experimental.pallas import tpu as pltpu
from jax.sharding import PartitionSpec as P

HD = 128
BLOCK = 128
NEGATIVE = -1e30
LOG2E = math.log2(math.e)
SCORE_SCALE = LOG2E / HD**0.5
BATCH = 4
LANES = 128
CUT_NUM, CUT_DEN = 1, 2

VMEM = pltpu.MemorySpace.VMEM
SMEM = pltpu.MemorySpace.SMEM


def in_vmem(count):
    return [pl.BlockSpec(memory_space=VMEM)] * count


def bf16(*shape):
    return jax.ShapeDtypeStruct(shape, jnp.bfloat16)


def f32(*shape):
    return jax.ShapeDtypeStruct(shape, jnp.float32)


def dot(left, right, contract=((1,), (0,))):
    return lax.dot_general(
        left, right, (contract, ((), ())), preferred_element_type=jnp.float32
    )


def pack(half, q, k, v, weight, kv_keep, kv_send, q_keep, q_send, left, sems):
    rows, width = q.shape
    part = width // 2
    mine = (lax.axis_index("seq") >= half).astype(jnp.int32)
    keep = pl.ds(pl.multiple_of(mine * part, part), part)
    send = pl.ds(pl.multiple_of((1 - mine) * part, part), part)
    copies = [
        (k.at[:, send], kv_send.at[:rows]),
        (v.at[:, send], kv_send.at[rows:]),
        (k.at[:, keep], kv_keep.at[:rows]),
        (v.at[:, keep], kv_keep.at[rows:]),
        (q.at[:, send], q_send),
        (q.at[:, keep], q_keep),
        (weight.at[:, : left.shape[1]], left),
    ]
    copies = [
        pltpu.make_async_copy(source, target, sems.at[n])
        for n, (source, target) in enumerate(copies)
    ]
    for copy in copies:
        copy.start()
    for copy in copies:
        copy.wait()


def attend(half, cores, places, first, last, *refs):
    mask, q_own, q_far = refs[:3]
    pieces = refs[3 : 3 + len(places)]
    rest = refs[3 + len(places) :]
    if not first:
        old_top, old_total, old_summed = rest[:3]
        rest = rest[3:]
    me = lax.axis_index("seq")
    rows = q_own.shape[0]
    blocks = rows // BLOCK
    heads = q_own.shape[1] // HD
    partner = me ^ half
    query_blocks = [me * blocks + a for a in range(blocks)]
    query_blocks += [partner * blocks + a for a in range(blocks)]
    bias = [
        [
            [
                jnp.where(mask[row, (me ^ place) * blocks + b] > 0, 0.0, NEGATIVE)
                for b in range(blocks)
            ]
            for row in query_blocks
        ]
        for place in places
    ]
    outs = []
    for head in range(heads):
        at = slice(head * HD, (head + 1) * HD)
        queries = jnp.concatenate([q_own[:, at], q_far[:, at]], axis=0)
        scores = []
        for n, piece in enumerate(pieces):
            raw = dot(queries, piece[:rows, at], ((1,), (1,)))
            scores.append(
                [
                    [
                        raw[a * BLOCK : (a + 1) * BLOCK, b * BLOCK : (b + 1) * BLOCK]
                        * SCORE_SCALE
                        + bias[n][a][b]
                        for b in range(blocks)
                    ]
                    for a in range(2 * blocks)
                ]
            )
        for a in range(2 * blocks):
            band = slice(a * BLOCK, (a + 1) * BLOCK)
            tiles = [piece[a][b] for piece in scores for b in range(blocks)]
            high = functools.reduce(jnp.maximum, tiles)
            top = jnp.max(high, axis=1, keepdims=True)
            if not first:
                before = old_top[band, at][:, :1]
                top = jnp.maximum(top, before)
                fade = jnp.exp2(before - top)
            weights = [jnp.exp2(tile - top) for tile in tiles]
            total = functools.reduce(jnp.add, weights)
            summed = None
            for n, piece in enumerate(pieces):
                mine = jnp.concatenate(weights[n * blocks : (n + 1) * blocks], axis=1)
                part = dot(mine.astype(jnp.bfloat16), piece[rows:, at])
                summed = part if summed is None else summed + part
            if not first:
                total = total + old_total[band, at] * fade
                summed = summed + old_summed[band, at] * fade
            if last:
                whole = jnp.sum(total, axis=1, keepdims=True)
                outs.append((summed / whole).astype(jnp.bfloat16))
            else:
                new_top, new_total, new_summed = rest
                new_top[band, at] = jnp.broadcast_to(top, (BLOCK, HD))
                new_total[band, at] = total
                new_summed[band, at] = summed
    if not last:
        return
    own_mine, own_other, far_mine, far_other = rest
    core = lax.rem(lax.axis_index("tp"), cores)
    chips = lax.axis_size("tp") // cores
    share = rows // (chips * cores)
    for head in range(heads):
        at = slice(head * HD, (head + 1) * HD)
        whole = jnp.concatenate(outs[head * 2 * blocks : (head + 1) * 2 * blocks], axis=0)
        for base, mine, other in ((0, own_mine, own_other), (rows, far_mine, far_other)):
            for chip in range(chips):
                start = base + chip * cores * share
                one = whole[start : start + share]
                two = whole[start + share : start + 2 * share]
                to = slice(chip * share, (chip + 1) * share)
                mine[to, at] = jnp.where(core == 0, one, two)
                other[to, at] = jnp.where(core == 0, two, one)


def stage(weight, right, sem):
    copy = pltpu.make_async_copy(weight.at[:, weight.shape[1] - right.shape[1] :], right, sem)
    copy.start()
    copy.wait()


def line_up(half, cores, own, far, other, far_other, *outs):
    low = lax.axis_index("seq") < half
    chips = len(outs)
    chip = lax.axis_index("tp") // cores
    share = own.shape[0] // chips
    part = own.shape[1]
    for step, out in enumerate(outs):
        place = lax.rem(chip + step, chips)
        rows = pl.ds(pl.multiple_of(place * share, share), share)
        one, two = own[rows], far[rows]
        out[:, :part] = jnp.where(low, one, two)
        out[:, part : 2 * part] = jnp.where(low, two, one)
        one, two = other[rows], far_other[rows]
        out[:, 2 * part : 3 * part] = jnp.where(low, one, two)
        out[:, 3 * part :] = jnp.where(low, two, one)


def project(attended, weight, core_weight, cut):
    rows = weight.shape[0]
    return dot(attended[:, :rows], weight[...]) + dot(attended[:, rows:], core_weight[:, cut])


def project_peers(cut, *refs):
    peers = len(refs) // 2 - 1
    right, core_weight = refs[peers : peers + 2]
    for attended, out in zip(refs[:peers], refs[peers + 2 :]):
        out[...] = project(attended, right, core_weight, slice(cut, None)).astype(jnp.bfloat16)


def project_own(cut, attended, left, right, core_weight, out_left, out_right):
    out_left[...] = project(attended, left, core_weight, slice(0, cut))
    out_right[...] = project(attended, right, core_weight, slice(cut, None))


def gated(residual, gate, branch):
    return (residual.astype(jnp.float32) + gate * branch).astype(jnp.bfloat16)


def finish_left(peers, cut, residual, gate, own, *refs):
    attended, weights, core_weights = refs[:peers], refs[peers : 2 * peers], refs[2 * peers : 3 * peers]
    out, block, sem = refs[3 * peers :]
    branch = own[...]
    for one, weight, core_weight in zip(attended, weights, core_weights):
        branch = branch + project(one, weight, core_weight, slice(None))
    block[...] = gated(residual[:, :cut], gate[:, :cut], branch)
    copy = pltpu.make_async_copy(block, out.at[:, :cut], sem)
    copy.start()
    copy.wait()


def finish_right(cut, residual, gate, own, *refs):
    peers, (_, out, block, sem) = refs[:-4], refs[-4:]
    branch = own[...]
    for peer in peers:
        branch = branch + peer[...].astype(jnp.float32)
    block[...] = gated(residual[:, cut:], gate[:, cut:], branch)
    copy = pltpu.make_async_copy(block, out.at[:, cut:], sem)
    copy.start()
    copy.wait()


def cost(microseconds):
    return pl.CostEstimate(flops=0, bytes_accessed=microseconds * 3_000_000, transcendentals=0)


def params(mib):
    return pltpu.CompilerParams(vmem_limit_bytes=mib * 2**20)


def shards(queries, keys, values, out_weight, residual, gate, block_mask):
    rows, width = queries.shape
    columns = out_weight.shape[1]
    seq, tp = lax.axis_size("seq"), lax.axis_size("tp")
    half = seq // 2
    cores = 2
    chips = tp // cores
    share = rows // tp
    part = width // 2
    peers = chips - 1
    cut = columns * CUT_NUM // CUT_DEN // LANES * LANES

    def swap(array, place):
        return lax.ppermute(array, "seq", [(i, i ^ place) for i in range(seq)])

    def across(array, place, core):
        return lax.ppermute(
            array,
            ("seq", "tp"),
            [
                (i * tp + t, (i ^ place) * tp + (t ^ core))
                for i in range(seq)
                for t in range(tp)
            ],
        )

    def swap_cores(array):
        return lax.ppermute(array, "tp", [(t, t ^ 1) for t in range(tp)])

    def to_chip(array, step):
        return lax.ppermute(
            array,
            "tp",
            [(t, (t // cores + step) % chips * cores + t % cores) for t in range(tp)],
        )

    def in_hbm(*arrays):
        return [pltpu.with_memory_space_constraint(array, pltpu.HBM) for array in arrays]

    kv_keep, kv_send, q_keep, q_send, left = pl.pallas_call(
        functools.partial(pack, half),
        out_shape=[bf16(2 * rows, part)] * 2 + [bf16(rows, part)] * 2 + [bf16(width, cut)],
        in_specs=[pl.BlockSpec(memory_space=pl.ANY)] * 4,
        out_specs=in_vmem(5),
        scratch_shapes=[pltpu.SemaphoreType.DMA((7,))],
        compiler_params=params(16),
        cost_estimate=cost(1),
        name="pack",
    )(*in_hbm(queries, keys, values, out_weight))
    kv_far = swap(kv_send, half)
    order = list(range(half - 1, 0, -1))
    direct = [m for m in order if m % 2 == 0 or m == 1]
    near = {m: swap(kv_keep, m) for m in direct}
    core_weight = swap_cores(out_weight)
    chip_weights = [to_chip(left, step) for step in range(1, chips)]
    kv_far, weight, q_send = lax.optimization_barrier((kv_far, out_weight, q_send))
    q_far = swap(q_send, half)
    far = {m: swap(kv_far, m) for m in order}
    for m in order:
        if m not in direct:
            near[m] = swap(near[m - 1], 1)
    right = pl.pallas_call(
        stage,
        out_shape=bf16(width, columns - cut),
        in_specs=[pl.BlockSpec(memory_space=pl.ANY)],
        out_specs=pl.BlockSpec(memory_space=VMEM),
        scratch_shapes=[pltpu.SemaphoreType.DMA],
        compiler_params=params(16),
        cost_estimate=cost(1),
        name="stage",
    )(*in_hbm(weight))
    pieces = [(0, kv_keep)] + [(m, near[m]) for m in order]
    pieces += [(half, kv_far)] + [(m ^ half, far[m]) for m in order]
    state = []
    for at in range(0, len(pieces), BATCH):
        batch = pieces[at : at + BATCH]
        first, last = at == 0, at + BATCH >= len(pieces)
        if last:
            out_shape = [bf16(rows // cores, part)] * 4
        else:
            out_shape = [f32(2 * rows, part)] * 3
        state = pl.pallas_call(
            functools.partial(attend, half, cores, [m for m, _ in batch], first, last),
            out_shape=out_shape,
            in_specs=[pl.BlockSpec(memory_space=SMEM)] + in_vmem(2 + len(batch) + len(state)),
            out_specs=in_vmem(len(out_shape)),
            compiler_params=params(32),
            cost_estimate=cost(2),
        name="attend",
        )(block_mask, q_keep, q_far, *[piece for _, piece in batch], *state)
    own_mine, own_other, far_mine, far_other = state
    from_far = across(far_mine, half, 0)
    from_far_core = across(far_other, half, 1)
    from_core = across(own_other, 0, 1)
    lined = pl.pallas_call(
        functools.partial(line_up, half, cores),
        out_shape=[bf16(share, cores * width)] * chips,
        in_specs=in_vmem(4),
        out_specs=in_vmem(chips),
        compiler_params=params(16),
        cost_estimate=cost(1),
        name="line_up",
    )(own_mine, from_far, from_core, from_far_core)
    arrived = [to_chip(array, step) for step, array in enumerate(lined[1:], 1)]
    sums = pl.pallas_call(
        functools.partial(project_peers, cut),
        out_shape=[bf16(share, columns - cut)] * peers,
        in_specs=in_vmem(peers + 2),
        out_specs=in_vmem(peers),
        compiler_params=params(32),
        cost_estimate=cost(1),
        name="project_peers",
    )(*lined[1:], right, core_weight)
    mine, *sums = lax.optimization_barrier((lined[0], *sums))
    own_left, own_right = pl.pallas_call(
        functools.partial(project_own, cut),
        out_shape=[f32(share, cut), f32(share, columns - cut)],
        in_specs=in_vmem(4),
        out_specs=in_vmem(2),
        compiler_params=params(32),
        cost_estimate=cost(1),
        name="project_own",
    )(mine, left, right, core_weight)
    summed = [to_chip(array, step) for step, array in enumerate(sums, 1)]
    own_left, *chip_weights = lax.optimization_barrier((own_left, *chip_weights))
    chip_core_weights = [swap_cores(weight) for weight in chip_weights]
    gate = gate[None, :]
    out = pl.pallas_call(
        functools.partial(finish_left, peers, cut),
        out_shape=bf16(share, columns),
        in_specs=in_vmem(3 + 3 * peers),
        out_specs=pl.BlockSpec(memory_space=pl.ANY),
        scratch_shapes=[pltpu.VMEM((share, cut), jnp.bfloat16), pltpu.SemaphoreType.DMA],
        compiler_params=params(32),
        cost_estimate=cost(2),
        name="finish_left",
    )(residual, gate, own_left, *arrived, *chip_weights, *chip_core_weights)
    return pl.pallas_call(
        functools.partial(finish_right, cut),
        out_shape=bf16(share, columns),
        in_specs=in_vmem(3 + peers) + [pl.BlockSpec(memory_space=pl.ANY)],
        out_specs=pl.BlockSpec(memory_space=pl.ANY),
        scratch_shapes=[
            pltpu.VMEM((share, columns - cut), jnp.bfloat16),
            pltpu.SemaphoreType.DMA,
        ],
        input_output_aliases={3 + peers: 0},
        compiler_params=params(16),
        cost_estimate=cost(1),
        name="finish_right",
    )(residual, gate, own_right, *summed, out)


def solution(mesh):
    return jax.shard_map(
        shards,
        mesh=mesh,
        in_specs=(
            P("seq", "tp"),
            P("seq", "tp"),
            P("seq", "tp"),
            P("tp", None),
            P(("seq", "tp"), None),
            P(),
            P(),
        ),
        out_specs=P(("seq", "tp"), None),
        check_vma=False,
    )
```

```python
import functools
import math

import jax
import jax.numpy as jnp
from jax import lax
from jax.experimental import pallas as pl
from jax.experimental.pallas import tpu as pltpu
from jax.sharding import PartitionSpec as P

HD = 128
BLOCK = 128
NEGATIVE = -1e30
LOG2E = math.log2(math.e)
SCORE_SCALE = LOG2E / HD**0.5
BATCH = 4
LANES = 128
CUT_NUM, CUT_DEN = 1, 2
HEAD_NUM, HEAD_DEN = 2, 3

VMEM = pltpu.MemorySpace.VMEM
SMEM = pltpu.MemorySpace.SMEM


def in_vmem(count):
    return [pl.BlockSpec(memory_space=VMEM)] * count


def bf16(*shape):
    return jax.ShapeDtypeStruct(shape, jnp.bfloat16)


def f32(*shape):
    return jax.ShapeDtypeStruct(shape, jnp.float32)


def dot(left, right, contract=((1,), (0,))):
    return lax.dot_general(
        left, right, (contract, ((), ())), preferred_element_type=jnp.float32
    )


def pack(half, q, k, v, weight, kv_keep, kv_send, q_keep, q_send, left, sems):
    rows, width = q.shape
    part = width // 2
    mine = (lax.axis_index("seq") >= half).astype(jnp.int32)
    keep = pl.ds(pl.multiple_of(mine * part, part), part)
    send = pl.ds(pl.multiple_of((1 - mine) * part, part), part)
    copies = [
        (k.at[:, send], kv_send.at[:rows]),
        (v.at[:, send], kv_send.at[rows:]),
        (k.at[:, keep], kv_keep.at[:rows]),
        (v.at[:, keep], kv_keep.at[rows:]),
        (q.at[:, send], q_send),
        (q.at[:, keep], q_keep),
        (weight.at[:, : left.shape[1]], left),
    ]
    copies = [
        pltpu.make_async_copy(source, target, sems.at[n])
        for n, (source, target) in enumerate(copies)
    ]
    for copy in copies:
        copy.start()
    for copy in copies:
        copy.wait()


def attend(queries, place, mask, pieces, state):
    rows = queries.shape[0]
    blocks = rows // BLOCK
    bias = [
        [
            [
                jnp.where(mask[place * blocks + a, owner * blocks + b] > 0, 0.0, NEGATIVE)
                for b in range(blocks)
            ]
            for a in range(blocks)
        ]
        for _, owner in pieces
    ]
    outs = {}
    for head in range(queries.shape[1] // HD):
        at = slice(head * HD, (head + 1) * HD)
        raw = [dot(queries[:, at], piece[:rows, at], ((1,), (1,))) for piece, _ in pieces]
        for a in range(blocks):
            band = slice(a * BLOCK, (a + 1) * BLOCK)
            tiles = [
                raw[n][band, b * BLOCK : (b + 1) * BLOCK] * SCORE_SCALE + bias[n][a][b]
                for n in range(len(pieces))
                for b in range(blocks)
            ]
            top = jnp.max(functools.reduce(jnp.maximum, tiles), axis=1, keepdims=True)
            if state is not None:
                old_top, old_total, old_summed = (ref[band, at] for ref in state)
                before = old_top[:, :1]
                top = jnp.maximum(top, before)
                fade = jnp.exp2(before - top)
            weights = [jnp.exp2(tile - top) for tile in tiles]
            total = functools.reduce(jnp.add, weights)
            summed = None
            for n, (piece, _) in enumerate(pieces):
                mine = jnp.concatenate(weights[n * blocks : (n + 1) * blocks], axis=1)
                part = dot(mine.astype(jnp.bfloat16), piece[rows:, at])
                summed = part if summed is None else summed + part
            if state is not None:
                total = total + old_total * fade
                summed = summed + old_summed * fade
            outs[head, a] = top, total, summed
    return outs


def keep_state(outs, refs):
    new_top, new_total, new_summed = refs
    for (head, a), (top, total, summed) in outs.items():
        where = (slice(a * BLOCK, (a + 1) * BLOCK), slice(head * HD, (head + 1) * HD))
        new_top[where] = jnp.broadcast_to(top, summed.shape)
        new_total[where] = total
        new_summed[where] = summed


def attend_near(places, first, mask, queries, *refs):
    me = lax.axis_index("seq")
    pieces = [(ref, me ^ place) for ref, place in zip(refs, places)]
    state = None if first else refs[len(places) : -3]
    keep_state(attend(queries, me, mask, pieces, state), refs[-3:])


def attend_rest(half, cores, places, first, last, mask, q_own, q_far, *refs):
    count = len(places)
    near, far = refs[:count], refs[count : 2 * count]
    own_state, rest = refs[2 * count : 2 * count + 3], refs[2 * count + 3 :]
    far_state = None
    if not first:
        far_state, rest = rest[:3], rest[3:]
    me = lax.axis_index("seq")
    near = [(ref, me ^ place) for ref, place in zip(near, places)]
    far = [(ref, me ^ half ^ place) for ref, place in zip(far, places)]
    for_far = attend(q_far, me ^ half, mask, near + far, far_state)
    for_own = attend(q_own, me, mask, far, own_state)
    if not last:
        keep_state(for_own, rest[:3])
        keep_state(for_far, rest[3:])
        return
    own_mine, own_other, far_mine, far_other = rest
    core = lax.rem(lax.axis_index("tp"), cores)
    chips = lax.axis_size("tp") // cores
    rows, width = q_own.shape
    share = rows // (chips * cores)
    for outs, mine, other in ((for_far, far_mine, far_other), (for_own, own_mine, own_other)):
        for head in range(width // HD):
            at = slice(head * HD, (head + 1) * HD)
            whole = []
            for a in range(rows // BLOCK):
                _, total, summed = outs[head, a]
                whole.append(
                    (summed / jnp.sum(total, axis=1, keepdims=True)).astype(jnp.bfloat16)
                )
            whole = jnp.concatenate(whole, axis=0)
            for chip in range(chips):
                start = chip * cores * share
                one = whole[start : start + share]
                two = whole[start + share : start + 2 * share]
                to = slice(chip * share, (chip + 1) * share)
                mine[to, at] = jnp.where(core == 0, one, two)
                other[to, at] = jnp.where(core == 0, two, one)


def stage(weight, right, sem):
    copy = pltpu.make_async_copy(weight.at[:, weight.shape[1] - right.shape[1] :], right, sem)
    copy.start()
    copy.wait()


def line_up(half, cores, own, far, other, far_other, *outs):
    low = lax.axis_index("seq") < half
    chips = len(outs)
    chip = lax.axis_index("tp") // cores
    share = own.shape[0] // chips
    part = own.shape[1]
    for step, out in enumerate(outs):
        place = lax.rem(chip + step, chips)
        rows = pl.ds(pl.multiple_of(place * share, share), share)
        one, two = own[rows], far[rows]
        out[:, :part] = jnp.where(low, one, two)
        out[:, part : 2 * part] = jnp.where(low, two, one)
        one, two = other[rows], far_other[rows]
        out[:, 2 * part : 3 * part] = jnp.where(low, one, two)
        out[:, 3 * part :] = jnp.where(low, two, one)


def project(attended, weight, core_weight, cut):
    rows = weight.shape[0]
    return dot(attended[:, :rows], weight[...]) + dot(attended[:, rows:], core_weight[:, cut])


def project_peers(cut, *refs):
    peers = (len(refs) - 2) // 3
    right, core_weight = refs[peers : peers + 2]
    outs = refs[peers + 2 :]
    for n, attended in enumerate(refs[:peers]):
        first, second = outs[2 * n : 2 * n + 2]
        rows = attended.shape[1]
        head = first.shape[1] - rows
        first[:, :rows] = attended[...]
        first[:, rows:] = project(
            attended, right.at[:, :head], core_weight, slice(cut, cut + head)
        ).astype(jnp.bfloat16)
        second[...] = project(
            attended, right.at[:, head:], core_weight, slice(cut + head, None)
        ).astype(jnp.bfloat16)


def project_own(cut, attended, left, right, core_weight, out_left, out_right):
    out_left[...] = project(attended, left, core_weight, slice(0, cut))
    out_right[...] = project(attended, right, core_weight, slice(cut, None))


def gated(residual, gate, branch):
    return (residual.astype(jnp.float32) + gate * branch).astype(jnp.bfloat16)


def write_out(block, out, columns, sem):
    copy = pltpu.make_async_copy(block, out.at[:, columns], sem)
    copy.start()
    copy.wait()


def finish_left(peers, cut, residual, gate, own_left, own_right, *refs):
    firsts, weights, core_weights = refs[:peers], refs[peers : 2 * peers], refs[2 * peers : 3 * peers]
    out, block, sem = refs[3 * peers :]
    end = block.shape[1]
    head = end - cut
    left, right = own_left[...], own_right[:, :head]
    for first, weight, core_weight in zip(firsts, weights, core_weights):
        rows = first.shape[1] - head
        left = left + project(first.at[:, :rows], weight, core_weight, slice(None))
        right = right + first[:, rows:].astype(jnp.float32)
    block[:, :cut] = gated(residual[:, :cut], gate[:, :cut], left)
    block[:, cut:] = gated(residual[:, cut:end], gate[:, cut:end], right)
    write_out(block, out, slice(0, end), sem)


def finish_right(residual, gate, own, *refs):
    seconds, (_, out, block, sem) = refs[:-4], refs[-4:]
    tail = block.shape[1]
    start = out.shape[1] - tail
    branch = own[:, own.shape[1] - tail :]
    for second in seconds:
        branch = branch + second[...].astype(jnp.float32)
    block[...] = gated(residual[:, start:], gate[:, start:], branch)
    write_out(block, out, slice(start, None), sem)


def cost(microseconds):
    return pl.CostEstimate(flops=0, bytes_accessed=microseconds * 3_000_000, transcendentals=0)


def params(mib):
    return pltpu.CompilerParams(vmem_limit_bytes=mib * 2**20)


def shards(queries, keys, values, out_weight, residual, gate, block_mask):
    rows, width = queries.shape
    columns = out_weight.shape[1]
    seq, tp = lax.axis_size("seq"), lax.axis_size("tp")
    half = seq // 2
    cores = 2
    chips = tp // cores
    share = rows // tp
    part = width // 2
    peers = chips - 1
    cut = columns * CUT_NUM // CUT_DEN // LANES * LANES
    head = (columns - cut) * HEAD_NUM // HEAD_DEN // LANES * LANES

    def swap(array, place):
        return lax.ppermute(array, "seq", [(i, i ^ place) for i in range(seq)])

    def across(array, place, core):
        return lax.ppermute(
            array,
            ("seq", "tp"),
            [
                (i * tp + t, (i ^ place) * tp + (t ^ core))
                for i in range(seq)
                for t in range(tp)
            ],
        )

    def swap_cores(array):
        return lax.ppermute(array, "tp", [(t, t ^ 1) for t in range(tp)])

    def to_chip(array, step):
        return lax.ppermute(
            array,
            "tp",
            [(t, (t // cores + step) % chips * cores + t % cores) for t in range(tp)],
        )

    def in_hbm(*arrays):
        return [pltpu.with_memory_space_constraint(array, pltpu.HBM) for array in arrays]

    kv_keep, kv_send, q_keep, q_send, left = pl.pallas_call(
        functools.partial(pack, half),
        out_shape=[bf16(2 * rows, part)] * 2 + [bf16(rows, part)] * 2 + [bf16(width, cut)],
        in_specs=[pl.BlockSpec(memory_space=pl.ANY)] * 4,
        out_specs=in_vmem(5),
        scratch_shapes=[pltpu.SemaphoreType.DMA((7,))],
        compiler_params=params(16),
        cost_estimate=cost(1),
        name="pack",
    )(*in_hbm(queries, keys, values, out_weight))
    kv_far = swap(kv_send, half)
    order = list(range(half - 1, 0, -1))
    direct = [m for m in order if m % 2 == 0 or m == 1]
    near = {m: swap(kv_keep, m) for m in direct}
    chip_weights = [to_chip(left, step) for step in range(1, chips)]
    core_weight = swap_cores(out_weight)
    kv_far, weight, q_send, core_weight = lax.optimization_barrier((kv_far, out_weight, q_send, core_weight))
    q_far = swap(q_send, half)
    far = {m: swap(kv_far, m) for m in order}
    for m in order:
        if m not in direct:
            near[m] = swap(near[m - 1], 1)
    right = pl.pallas_call(
        stage,
        out_shape=bf16(width, columns - cut),
        in_specs=[pl.BlockSpec(memory_space=pl.ANY)],
        out_specs=pl.BlockSpec(memory_space=VMEM),
        scratch_shapes=[pltpu.SemaphoreType.DMA],
        compiler_params=params(16),
        cost_estimate=cost(1),
        name="stage",
    )(*in_hbm(weight))
    near[0], far[0] = kv_keep, kv_far
    places = [0] + order
    batches = [places[at : at + BATCH] for at in range(0, len(places), BATCH)]
    smem = pl.BlockSpec(memory_space=SMEM)
    own_state = []
    for at, batch in enumerate(batches):
        own_state = pl.pallas_call(
            functools.partial(attend_near, batch, at == 0),
            out_shape=[f32(rows, part)] * 3,
            in_specs=[smem] + in_vmem(1 + len(batch) + len(own_state)),
            out_specs=in_vmem(3),
            compiler_params=params(32),
            cost_estimate=cost(1),
            name="attend_near",
        )(block_mask, q_keep, *[near[m] for m in batch], *own_state)
    far_state = []
    for at, batch in enumerate(batches):
        last = at == len(batches) - 1
        state = [*own_state, *far_state]
        out_shape = [bf16(rows // cores, part)] * 4 if last else [f32(rows, part)] * 6
        outs = pl.pallas_call(
            functools.partial(attend_rest, half, cores, batch, at == 0, last),
            out_shape=out_shape,
            in_specs=[smem] + in_vmem(2 + 2 * len(batch) + len(state)),
            out_specs=in_vmem(len(out_shape)),
            compiler_params=params(32),
            cost_estimate=cost(3),
            name="attend_rest",
        )(block_mask, q_keep, q_far, *[near[m] for m in batch], *[far[m] for m in batch], *state)
        own_state, far_state = outs[:3], outs[3:]
    own_mine, own_other, far_mine, far_other = outs
    from_far = across(far_mine, half, 0)
    from_far_core = across(far_other, half, 1)
    from_core = across(own_other, 0, 1)
    lined = pl.pallas_call(
        functools.partial(line_up, half, cores),
        out_shape=[bf16(share, cores * width)] * chips,
        in_specs=in_vmem(4),
        out_specs=in_vmem(chips),
        compiler_params=params(16),
        cost_estimate=cost(1),
        name="line_up",
    )(own_mine, from_far, from_core, from_far_core)
    sums = pl.pallas_call(
        functools.partial(project_peers, cut),
        out_shape=[bf16(share, cores * width + head), bf16(share, columns - cut - head)] * peers,
        in_specs=in_vmem(peers + 2),
        out_specs=in_vmem(2 * peers),
        compiler_params=params(32),
        cost_estimate=cost(1),
        name="project_peers",
    )(*lined[1:], right, core_weight)
    mine, *sums = lax.optimization_barrier((lined[0], *sums))
    own_left, own_right = pl.pallas_call(
        functools.partial(project_own, cut),
        out_shape=[f32(share, cut), f32(share, columns - cut)],
        in_specs=in_vmem(4),
        out_specs=in_vmem(2),
        compiler_params=params(32),
        cost_estimate=cost(1),
        name="project_own",
    )(mine, left, right, core_weight)
    sums, chip_weights = lax.optimization_barrier((sums, chip_weights))
    firsts = [to_chip(array, step) for step, array in enumerate(sums[::2], 1)]
    seconds = [to_chip(array, step) for step, array in enumerate(sums[1::2], 1)]
    chip_core_weights = [swap_cores(weight) for weight in chip_weights]
    gate = gate[None, :]
    out = pl.pallas_call(
        functools.partial(finish_left, peers, cut),
        out_shape=bf16(share, columns),
        in_specs=in_vmem(4 + 3 * peers),
        out_specs=pl.BlockSpec(memory_space=pl.ANY),
        scratch_shapes=[pltpu.VMEM((share, cut + head), jnp.bfloat16), pltpu.SemaphoreType.DMA],
        compiler_params=params(32),
        cost_estimate=cost(2),
        name="finish_left",
    )(residual, gate, own_left, own_right, *firsts, *chip_weights, *chip_core_weights)
    return pl.pallas_call(
        finish_right,
        out_shape=bf16(share, columns),
        in_specs=in_vmem(3 + peers) + [pl.BlockSpec(memory_space=pl.ANY)],
        out_specs=pl.BlockSpec(memory_space=pl.ANY),
        scratch_shapes=[
            pltpu.VMEM((share, columns - cut - head), jnp.bfloat16),
            pltpu.SemaphoreType.DMA,
        ],
        input_output_aliases={3 + peers: 0},
        compiler_params=params(16),
        cost_estimate=cost(1),
        name="finish_right",
    )(residual, gate, own_right, *seconds, out)


def solution(mesh):
    return jax.shard_map(
        shards,
        mesh=mesh,
        in_specs=(
            P("seq", "tp"),
            P("seq", "tp"),
            P("seq", "tp"),
            P("tp", None),
            P(("seq", "tp"), None),
            P(),
            P(),
        ),
        out_specs=P(("seq", "tp"), None),
        check_vma=False,
    )
```

```python
import functools
import math

import jax
import jax.numpy as jnp
from jax import lax
from jax.experimental import pallas as pl
from jax.experimental.pallas import tpu as pltpu
from jax.sharding import PartitionSpec as P

HD = 128
BLOCK = 128
NEGATIVE = -1e30
LOG2E = math.log2(math.e)
SCORE_SCALE = LOG2E / HD**0.5
BATCH = 4
LANES = 128
CUT_NUM, CUT_DEN = 1, 2
HEAD_NUM, HEAD_DEN = 1, 3

VMEM = pltpu.MemorySpace.VMEM
SMEM = pltpu.MemorySpace.SMEM


def in_vmem(count):
    return [pl.BlockSpec(memory_space=VMEM)] * count


def bf16(*shape):
    return jax.ShapeDtypeStruct(shape, jnp.bfloat16)


def f32(*shape):
    return jax.ShapeDtypeStruct(shape, jnp.float32)


def dot(left, right, contract=((1,), (0,))):
    return lax.dot_general(
        left, right, (contract, ((), ())), preferred_element_type=jnp.float32
    )


def pack(half, q, k, v, weight, kv_keep, kv_send, q_keep, q_send, left, sems):
    rows, width = q.shape
    part = width // 2
    mine = (lax.axis_index("seq") >= half).astype(jnp.int32)
    keep = pl.ds(pl.multiple_of(mine * part, part), part)
    send = pl.ds(pl.multiple_of((1 - mine) * part, part), part)
    copies = [
        (k.at[:, send], kv_send.at[:rows]),
        (v.at[:, send], kv_send.at[rows:]),
        (k.at[:, keep], kv_keep.at[:rows]),
        (v.at[:, keep], kv_keep.at[rows:]),
        (q.at[:, send], q_send),
        (q.at[:, keep], q_keep),
        (weight.at[:, : left.shape[1]], left),
    ]
    copies = [
        pltpu.make_async_copy(source, target, sems.at[n])
        for n, (source, target) in enumerate(copies)
    ]
    for copy in copies:
        copy.start()
    for copy in copies:
        copy.wait()


def attend(queries, first_row, bias, pieces, state):
    rows = queries.shape[0]
    blocks = rows // BLOCK
    outs = {}
    for head in range(queries.shape[1] // HD):
        at = slice(head * HD, (head + 1) * HD)
        raw = [dot(queries[:, at], piece[:rows, at], ((1,), (1,))) for piece, _ in pieces]
        for a in range(blocks):
            band = slice(a * BLOCK, (a + 1) * BLOCK)
            tiles = []
            for n, (_, place) in enumerate(pieces):
                for b in range(blocks):
                    row = (first_row + a) * bias.shape[0] // (2 * blocks) + place * blocks + b
                    tile = raw[n][band, b * BLOCK : (b + 1) * BLOCK]
                    tiles.append(tile * SCORE_SCALE + bias[row : row + 1, :])
            top = jnp.max(functools.reduce(jnp.maximum, tiles), axis=1, keepdims=True)
            if state is not None:
                old_top, old_total, old_summed = (ref[band, at] for ref in state)
                before = old_top[:, :1]
                top = jnp.maximum(top, before)
                fade = jnp.exp2(before - top)
            weights = [jnp.exp2(tile - top) for tile in tiles]
            total = functools.reduce(jnp.add, weights)
            summed = None
            for n, (piece, _) in enumerate(pieces):
                mine = jnp.concatenate(weights[n * blocks : (n + 1) * blocks], axis=1)
                part = dot(mine.astype(jnp.bfloat16), piece[rows:, at])
                summed = part if summed is None else summed + part
            if state is not None:
                total = total + old_total * fade
                summed = summed + old_summed * fade
            outs[head, a] = top, total, summed
    return outs


def keep_state(outs, refs):
    new_top, new_total, new_summed = refs
    for (head, a), (top, total, summed) in outs.items():
        where = (slice(a * BLOCK, (a + 1) * BLOCK), slice(head * HD, (head + 1) * HD))
        new_top[where] = jnp.broadcast_to(top, summed.shape)
        new_total[where] = total
        new_summed[where] = summed


def attend_first(half, places, mask, queries, *refs):
    bias, state = refs[-4], refs[-3:]
    me = lax.axis_index("seq")
    blocks = queries.shape[0] // BLOCK
    keys = bias.shape[0] // (2 * blocks)
    for a in range(2 * blocks):
        row = (me if a < blocks else me ^ half) * blocks + a % blocks
        for b in range(keys):
            column = (me ^ (b // blocks)) * blocks + b % blocks
            allowed = jnp.where(mask[row, column] > 0, 0.0, NEGATIVE)
            bias[a * keys + b : a * keys + b + 1, :] = jnp.full((1, BLOCK), allowed, jnp.float32)
    keep_state(attend(queries, 0, bias, list(zip(refs, places)), None), state)


def attend_more(first_row, cores, places, last, stateful, bias, queries, *refs):
    pieces, rest = list(zip(refs, places)), refs[len(places) :]
    state = None
    if stateful:
        state, rest = rest[:3], rest[3:]
    outs = attend(queries, first_row, bias, pieces, state)
    if not last:
        keep_state(outs, rest)
        return
    mine, other = rest
    core = lax.rem(lax.axis_index("tp"), cores)
    chips = lax.axis_size("tp") // cores
    rows, width = queries.shape
    share = rows // (chips * cores)
    for head in range(width // HD):
        at = slice(head * HD, (head + 1) * HD)
        whole = []
        for a in range(rows // BLOCK):
            _, total, summed = outs[head, a]
            whole.append((summed / jnp.sum(total, axis=1, keepdims=True)).astype(jnp.bfloat16))
        whole = jnp.concatenate(whole, axis=0)
        for chip in range(chips):
            start = chip * cores * share
            one = whole[start : start + share]
            two = whole[start + share : start + 2 * share]
            to = slice(chip * share, (chip + 1) * share)
            mine[to, at] = jnp.where(core == 0, one, two)
            other[to, at] = jnp.where(core == 0, two, one)


def stage(weight, right, sem):
    copy = pltpu.make_async_copy(weight.at[:, weight.shape[1] - right.shape[1] :], right, sem)
    copy.start()
    copy.wait()


def line_up(half, cores, own, far, other, far_other, *outs):
    low = lax.axis_index("seq") < half
    chips = len(outs)
    chip = lax.axis_index("tp") // cores
    share = own.shape[0] // chips
    part = own.shape[1]
    for step, out in enumerate(outs):
        place = lax.rem(chip + step, chips)
        rows = pl.ds(pl.multiple_of(place * share, share), share)
        one, two = own[rows], far[rows]
        out[:, :part] = jnp.where(low, one, two)
        out[:, part : 2 * part] = jnp.where(low, two, one)
        one, two = other[rows], far_other[rows]
        out[:, 2 * part : 3 * part] = jnp.where(low, one, two)
        out[:, 3 * part :] = jnp.where(low, two, one)


def project(attended, weight, core_weight, cut):
    rows = weight.shape[0]
    return dot(attended[:, :rows], weight[...]) + dot(attended[:, rows:], core_weight[:, cut])


def project_peers(cut, *refs):
    peers = (len(refs) - 2) // 3
    right, core_weight = refs[peers : peers + 2]
    outs = refs[peers + 2 :]
    for n, attended in enumerate(refs[:peers]):
        first, second = outs[2 * n : 2 * n + 2]
        rows = attended.shape[1]
        head = first.shape[1] - rows
        first[:, :rows] = attended[...]
        first[:, rows:] = project(
            attended, right.at[:, :head], core_weight, slice(cut, cut + head)
        ).astype(jnp.bfloat16)
        second[...] = project(
            attended, right.at[:, head:], core_weight, slice(cut + head, None)
        ).astype(jnp.bfloat16)


def project_own(cut, attended, left, right, core_weight, out_left, out_right):
    out_left[...] = project(attended, left, core_weight, slice(0, cut))
    out_right[...] = project(attended, right, core_weight, slice(cut, None))


def gated(residual, gate, branch):
    return (residual.astype(jnp.float32) + gate * branch).astype(jnp.bfloat16)


def write_out(block, out, columns, sem):
    copy = pltpu.make_async_copy(block, out.at[:, columns], sem)
    copy.start()
    copy.wait()


def finish_head(residual, gate, own_right, *refs):
    firsts, (out, block, sem) = refs[:-3], refs[-3:]
    head = block.shape[1]
    cut = out.shape[1] - own_right.shape[1]
    branch = own_right[:, :head]
    for first in firsts:
        branch = branch + first[:, first.shape[1] - head :].astype(jnp.float32)
    columns = slice(cut, cut + head)
    block[...] = gated(residual[:, columns], gate[:, columns], branch)
    write_out(block, out, columns, sem)


def finish_left(peers, cut, residual, gate, own, *refs):
    firsts, weights, core_weights = refs[:peers], refs[peers : 2 * peers], refs[2 * peers : 3 * peers]
    _, out, block, sem = refs[3 * peers :]
    branch = own[...]
    for first, weight, core_weight in zip(firsts, weights, core_weights):
        rows = 2 * weight.shape[0]
        branch = branch + project(first.at[:, :rows], weight, core_weight, slice(None))
    block[...] = gated(residual[:, :cut], gate[:, :cut], branch)
    write_out(block, out, slice(0, cut), sem)


def finish_right(residual, gate, own, *refs):
    seconds, (_, out, block, sem) = refs[:-4], refs[-4:]
    tail = block.shape[1]
    start = out.shape[1] - tail
    branch = own[:, own.shape[1] - tail :]
    for second in seconds:
        branch = branch + second[...].astype(jnp.float32)
    block[...] = gated(residual[:, start:], gate[:, start:], branch)
    write_out(block, out, slice(start, None), sem)


def cost(microseconds):
    return pl.CostEstimate(
        flops=int(microseconds * 1_000_000_000), bytes_accessed=0, transcendentals=0
    )


def params(mib):
    return pltpu.CompilerParams(vmem_limit_bytes=mib * 2**20)


def shards(queries, keys, values, out_weight, residual, gate, block_mask):
    rows, width = queries.shape
    columns = out_weight.shape[1]
    seq, tp = lax.axis_size("seq"), lax.axis_size("tp")
    half = seq // 2
    cores = 2
    chips = tp // cores
    share = rows // tp
    part = width // 2
    peers = chips - 1
    cut = columns * CUT_NUM // CUT_DEN // LANES * LANES
    head = (columns - cut) * HEAD_NUM // HEAD_DEN // LANES * LANES

    def swap(array, place):
        return lax.ppermute(array, "seq", [(i, i ^ place) for i in range(seq)])

    def across(array, place, core):
        return lax.ppermute(
            array,
            ("seq", "tp"),
            [
                (i * tp + t, (i ^ place) * tp + (t ^ core))
                for i in range(seq)
                for t in range(tp)
            ],
        )

    def swap_cores(array):
        return lax.ppermute(array, "tp", [(t, t ^ 1) for t in range(tp)])

    def to_chip(array, step):
        return lax.ppermute(
            array,
            "tp",
            [(t, (t // cores + step) % chips * cores + t % cores) for t in range(tp)],
        )

    def in_hbm(*arrays):
        return [pltpu.with_memory_space_constraint(array, pltpu.HBM) for array in arrays]

    kv_keep, kv_send, q_keep, q_send, left = pl.pallas_call(
        functools.partial(pack, half),
        out_shape=[bf16(2 * rows, part)] * 2 + [bf16(rows, part)] * 2 + [bf16(width, cut)],
        in_specs=[pl.BlockSpec(memory_space=pl.ANY)] * 4,
        out_specs=in_vmem(5),
        scratch_shapes=[pltpu.SemaphoreType.DMA((7,))],
        compiler_params=params(16),
        cost_estimate=cost(1.6),
        name="pack",
    )(*in_hbm(queries, keys, values, out_weight))
    kv_far = swap(kv_send, half)
    order = sorted(range(1, half), key=lambda m: (m.bit_count(), -m))
    direct = [m for m in order if m % 2 == 0 or m == 1]
    near = {m: swap(kv_keep, m) for m in direct}
    chip_weights = [to_chip(left, step) for step in range(1, chips)]
    core_weight = swap_cores(out_weight)
    kv_far, weight, q_send, core_weight = lax.optimization_barrier((kv_far, out_weight, q_send, core_weight))
    q_far = swap(q_send, half)
    far = {m: swap(kv_far, m) for m in order}
    for m in order:
        if m not in direct:
            near[m] = swap(near[m - 1], 1)
    right = pl.pallas_call(
        stage,
        out_shape=bf16(width, columns - cut),
        in_specs=[pl.BlockSpec(memory_space=pl.ANY)],
        out_specs=pl.BlockSpec(memory_space=VMEM),
        scratch_shapes=[pltpu.SemaphoreType.DMA],
        compiler_params=params(16),
        cost_estimate=cost(1.3),
        name="stage",
    )(*in_hbm(weight))
    near[0], far[0] = kv_keep, kv_far
    places = [0] + order
    batches = [places[at : at + BATCH] for at in range(0, len(places), BATCH)]
    blocks = rows // BLOCK
    state_shape = [f32(rows, part)] * 3

    def attend_all(first_row, queries, batches, state, microseconds):
        for at, pieces in enumerate(batches):
            last = at == len(batches) - 1
            out_shape = [bf16(rows // cores, part)] * 2 if last else state_shape
            held = [place for place, _ in pieces]
            state = pl.pallas_call(
                functools.partial(attend_more, first_row, cores, held, last, bool(state)),
                out_shape=out_shape,
                in_specs=in_vmem(2 + len(pieces) + len(state)),
                out_specs=in_vmem(len(out_shape)),
                compiler_params=params(32),
                cost_estimate=cost(microseconds),
                name="attend_far" if first_row else "attend_own",
            )(bias, queries, *[array for _, array in pieces], *state)
        return state

    bias, *own_state = pl.pallas_call(
        functools.partial(attend_first, half, batches[0]),
        out_shape=[f32(2 * blocks * seq * blocks, BLOCK)] + state_shape,
        in_specs=[pl.BlockSpec(memory_space=SMEM)] + in_vmem(1 + len(batches[0])),
        out_specs=in_vmem(4),
        compiler_params=params(32),
        cost_estimate=cost(1.3),
        name="attend_near",
    )(block_mask, q_keep, *[near[m] for m in batches[0]])
    near_batches = [[(m, near[m]) for m in batch] for batch in batches]
    far_batches = [[(m ^ half, far[m]) for m in batch] for batch in batches]
    both = [one + two for one, two in zip(near_batches, far_batches)]
    far_mine, far_other = attend_all(blocks, q_far, both, [], 2)
    own_mine, own_other = attend_all(0, q_keep, near_batches[1:] + far_batches, own_state, 1)
    from_far = across(far_mine, half, 0)
    from_far_core = across(far_other, half, 1)
    from_core = across(own_other, 0, 1)
    lined = pl.pallas_call(
        functools.partial(line_up, half, cores),
        out_shape=[bf16(share, cores * width)] * chips,
        in_specs=in_vmem(4),
        out_specs=in_vmem(chips),
        compiler_params=params(16),
        cost_estimate=cost(0.1),
        name="line_up",
    )(own_mine, from_far, from_core, from_far_core)
    sums = pl.pallas_call(
        functools.partial(project_peers, cut),
        out_shape=[bf16(share, cores * width + head), bf16(share, columns - cut - head)] * peers,
        in_specs=in_vmem(peers + 2),
        out_specs=in_vmem(2 * peers),
        compiler_params=params(32),
        cost_estimate=cost(0.5),
        name="project_peers",
    )(*lined[1:], right, core_weight)
    mine, chip_weights, *_ = lax.optimization_barrier((lined[0], chip_weights, *sums))
    own_left, own_right = pl.pallas_call(
        functools.partial(project_own, cut),
        out_shape=[f32(share, cut), f32(share, columns - cut)],
        in_specs=in_vmem(4),
        out_specs=in_vmem(2),
        compiler_params=params(32),
        cost_estimate=cost(0.1),
        name="project_own",
    )(mine, left, right, core_weight)
    firsts = [to_chip(array, step) for step, array in enumerate(sums[::2], 1)]
    seconds = [to_chip(array, step) for step, array in enumerate(sums[1::2], 1)]
    chip_core_weights = [swap_cores(weight) for weight in chip_weights]
    gate = gate[None, :]
    anywhere = pl.BlockSpec(memory_space=pl.ANY)
    out = pl.pallas_call(
        finish_head,
        out_shape=bf16(share, columns),
        in_specs=in_vmem(3 + peers),
        out_specs=anywhere,
        scratch_shapes=[pltpu.VMEM((share, head), jnp.bfloat16), pltpu.SemaphoreType.DMA],
        compiler_params=params(16),
        cost_estimate=cost(20),
        name="finish_head",
    )(residual, gate, own_right, *firsts)
    out = pl.pallas_call(
        functools.partial(finish_left, peers, cut),
        out_shape=bf16(share, columns),
        in_specs=in_vmem(3 + 3 * peers) + [anywhere],
        out_specs=anywhere,
        scratch_shapes=[pltpu.VMEM((share, cut), jnp.bfloat16), pltpu.SemaphoreType.DMA],
        input_output_aliases={3 + 3 * peers: 0},
        compiler_params=params(32),
        cost_estimate=cost(1.5),
        name="finish_left",
    )(residual, gate, own_left, *firsts, *chip_weights, *chip_core_weights, out)
    return pl.pallas_call(
        finish_right,
        out_shape=bf16(share, columns),
        in_specs=in_vmem(3 + peers) + [pl.BlockSpec(memory_space=pl.ANY)],
        out_specs=pl.BlockSpec(memory_space=pl.ANY),
        scratch_shapes=[
            pltpu.VMEM((share, columns - cut - head), jnp.bfloat16),
            pltpu.SemaphoreType.DMA,
        ],
        input_output_aliases={3 + peers: 0},
        compiler_params=params(16),
        cost_estimate=cost(0.7),
        name="finish_right",
    )(residual, gate, own_right, *seconds, out)


def solution(mesh):
    return jax.shard_map(
        shards,
        mesh=mesh,
        in_specs=(
            P("seq", "tp"),
            P("seq", "tp"),
            P("seq", "tp"),
            P("tp", None),
            P(("seq", "tp"), None),
            P(),
            P(),
        ),
        out_specs=P(("seq", "tp"), None),
        check_vma=False,
    )
```

```python
import functools
import math

import jax
import jax.numpy as jnp
from jax import lax
from jax.experimental import pallas as pl
from jax.experimental.pallas import tpu as pltpu
from jax.sharding import PartitionSpec as P

HD = 128
BLOCK = 128
NEGATIVE = -1e30
LOG2E = math.log2(math.e)
SCORE_SCALE = LOG2E / HD**0.5
BATCH = 4
LANES = 128
CUT_NUM, CUT_DEN = 12, 25
HEAD_NUM, HEAD_DEN = 1, 3

VMEM = pltpu.MemorySpace.VMEM
SMEM = pltpu.MemorySpace.SMEM


def in_vmem(count):
    return [pl.BlockSpec(memory_space=VMEM)] * count


def bf16(*shape):
    return jax.ShapeDtypeStruct(shape, jnp.bfloat16)


def f32(*shape):
    return jax.ShapeDtypeStruct(shape, jnp.float32)


def dot(left, right, contract=((1,), (0,))):
    return lax.dot_general(
        left, right, (contract, ((), ())), preferred_element_type=jnp.float32
    )


def pack(half, q, k, v, weight, kv_keep, kv_send, q_keep, q_send, left, sems):
    rows, width = q.shape
    part = width // 2
    mine = (lax.axis_index("seq") >= half).astype(jnp.int32)
    keep = pl.ds(pl.multiple_of(mine * part, part), part)
    send = pl.ds(pl.multiple_of((1 - mine) * part, part), part)
    copies = [
        (k.at[:, send], kv_send.at[:rows]),
        (v.at[:, send], kv_send.at[rows:]),
        (k.at[:, keep], kv_keep.at[:rows]),
        (v.at[:, keep], kv_keep.at[rows:]),
        (q.at[:, send], q_send),
        (q.at[:, keep], q_keep),
        (weight.at[:, : left.shape[1]], left),
    ]
    copies = [
        pltpu.make_async_copy(source, target, sems.at[n])
        for n, (source, target) in enumerate(copies)
    ]
    for copy in copies:
        copy.start()
    for copy in copies:
        copy.wait()


def attend(queries, first_row, bias, pieces, state):
    rows = queries.shape[0]
    blocks = rows // BLOCK
    outs = {}
    for head in range(queries.shape[1] // HD):
        at = slice(head * HD, (head + 1) * HD)
        raw = [dot(queries[:, at], piece[:rows, at], ((1,), (1,))) for piece, _ in pieces]
        for a in range(blocks):
            band = slice(a * BLOCK, (a + 1) * BLOCK)
            tiles = []
            for n, (_, place) in enumerate(pieces):
                for b in range(blocks):
                    row = (first_row + a) * bias.shape[0] // (2 * blocks) + place * blocks + b
                    tile = raw[n][band, b * BLOCK : (b + 1) * BLOCK]
                    tiles.append(tile * SCORE_SCALE + bias[row : row + 1, :])
            top = jnp.max(functools.reduce(jnp.maximum, tiles), axis=1, keepdims=True)
            if state is not None:
                old_top, old_total, old_summed = (ref[band, at] for ref in state)
                before = old_top[:, :1]
                top = jnp.maximum(top, before)
                fade = jnp.exp2(before - top)
            weights = [jnp.exp2(tile - top) for tile in tiles]
            total = functools.reduce(jnp.add, weights)
            summed = None
            for n, (piece, _) in enumerate(pieces):
                mine = jnp.concatenate(weights[n * blocks : (n + 1) * blocks], axis=1)
                part = dot(mine.astype(jnp.bfloat16), piece[rows:, at])
                summed = part if summed is None else summed + part
            if state is not None:
                total = total + old_total * fade
                summed = summed + old_summed * fade
            outs[head, a] = top, total, summed
    return outs


def keep_state(outs, refs):
    new_top, new_total, new_summed = refs
    for (head, a), (top, total, summed) in outs.items():
        where = (slice(a * BLOCK, (a + 1) * BLOCK), slice(head * HD, (head + 1) * HD))
        new_top[where] = jnp.broadcast_to(top, summed.shape)
        new_total[where] = total
        new_summed[where] = summed


def attend_first(half, places, mask, queries, *refs):
    bias, state = refs[-4], refs[-3:]
    me = lax.axis_index("seq")
    blocks = queries.shape[0] // BLOCK
    keys = bias.shape[0] // (2 * blocks)
    for a in range(2 * blocks):
        row = (me if a < blocks else me ^ half) * blocks + a % blocks
        for b in range(keys):
            column = (me ^ (b // blocks)) * blocks + b % blocks
            allowed = jnp.where(mask[row, column] > 0, 0.0, NEGATIVE)
            bias[a * keys + b : a * keys + b + 1, :] = jnp.full((1, BLOCK), allowed, jnp.float32)
    keep_state(attend(queries, 0, bias, list(zip(refs, places)), None), state)


def attend_more(first_row, cores, places, last, stateful, bias, queries, *refs):
    pieces, rest = list(zip(refs, places)), refs[len(places) :]
    state = None
    if stateful:
        state, rest = rest[:3], rest[3:]
    outs = attend(queries, first_row, bias, pieces, state)
    if not last:
        keep_state(outs, rest)
        return
    mine, other = rest
    core = lax.rem(lax.axis_index("tp"), cores)
    chips = lax.axis_size("tp") // cores
    rows, width = queries.shape
    share = rows // (chips * cores)
    for head in range(width // HD):
        at = slice(head * HD, (head + 1) * HD)
        whole = []
        for a in range(rows // BLOCK):
            _, total, summed = outs[head, a]
            whole.append((summed / jnp.sum(total, axis=1, keepdims=True)).astype(jnp.bfloat16))
        whole = jnp.concatenate(whole, axis=0)
        for chip in range(chips):
            start = chip * cores * share
            one = whole[start : start + share]
            two = whole[start + share : start + 2 * share]
            to = slice(chip * share, (chip + 1) * share)
            mine[to, at] = jnp.where(core == 0, one, two)
            other[to, at] = jnp.where(core == 0, two, one)


def stage(weight, right, sem):
    copy = pltpu.make_async_copy(weight.at[:, weight.shape[1] - right.shape[1] :], right, sem)
    copy.start()
    copy.wait()


def line_up(half, cores, own, far_other, other, far, *outs):
    low = lax.axis_index("seq") < half
    chips = len(outs)
    chip = lax.axis_index("tp") // cores
    share = own.shape[0] // chips
    part = own.shape[1]
    for step, out in enumerate(outs):
        place = lax.rem(chip + step, chips)
        rows = pl.ds(pl.multiple_of(place * share, share), share)
        one, two = own[rows], far[rows]
        out[:, :part] = jnp.where(low, one, two)
        out[:, part : 2 * part] = jnp.where(low, two, one)
        one, two = other[rows], far_other[rows]
        out[:, 2 * part : 3 * part] = jnp.where(low, one, two)
        out[:, 3 * part :] = jnp.where(low, two, one)


def project(attended, weight, core_weight, cut):
    rows = weight.shape[0]
    return dot(attended[:, :rows], weight[...]) + dot(attended[:, rows:], core_weight[:, cut])


def project_peers(cut, *refs):
    peers = (len(refs) - 2) // 3
    right, core_weight = refs[peers : peers + 2]
    outs = refs[peers + 2 :]
    for n, attended in enumerate(refs[:peers]):
        first, second = outs[2 * n : 2 * n + 2]
        rows = attended.shape[1]
        head = first.shape[1] - rows
        first[:, :rows] = attended[...]
        first[:, rows:] = project(
            attended, right.at[:, :head], core_weight, slice(cut, cut + head)
        ).astype(jnp.bfloat16)
        second[...] = project(
            attended, right.at[:, head:], core_weight, slice(cut + head, None)
        ).astype(jnp.bfloat16)


def project_own(cut, attended, left, right, core_weight, out_left, out_right):
    out_left[...] = project(attended, left, core_weight, slice(0, cut))
    out_right[...] = project(attended, right, core_weight, slice(cut, None))


def gated(residual, gate, branch):
    return (residual.astype(jnp.float32) + gate * branch).astype(jnp.bfloat16)


def write_out(block, out, columns, sem):
    copy = pltpu.make_async_copy(block, out.at[:, columns], sem)
    copy.start()
    copy.wait()


def finish_head(residual, gate, own_right, *refs):
    firsts, (out, block, sem) = refs[:-3], refs[-3:]
    head = block.shape[1]
    cut = out.shape[1] - own_right.shape[1]
    branch = own_right[:, :head]
    for first in firsts:
        branch = branch + first[:, first.shape[1] - head :].astype(jnp.float32)
    columns = slice(cut, cut + head)
    block[...] = gated(residual[:, columns], gate[:, columns], branch)
    write_out(block, out, columns, sem)


def finish_left(peers, cut, residual, gate, own, *refs):
    firsts, weights, core_weights = refs[:peers], refs[peers : 2 * peers], refs[2 * peers : 3 * peers]
    _, out, block, sem = refs[3 * peers :]
    branch = own[...]
    for first, weight, core_weight in zip(firsts, weights, core_weights):
        rows = 2 * weight.shape[0]
        branch = branch + project(first.at[:, :rows], weight, core_weight, slice(None))
    block[...] = gated(residual[:, :cut], gate[:, :cut], branch)
    write_out(block, out, slice(0, cut), sem)


def finish_right(residual, gate, own, *refs):
    seconds, (_, out, block, sem) = refs[:-4], refs[-4:]
    tail = block.shape[1]
    start = out.shape[1] - tail
    branch = own[:, own.shape[1] - tail :]
    for second in seconds:
        branch = branch + second[...].astype(jnp.float32)
    block[...] = gated(residual[:, start:], gate[:, start:], branch)
    write_out(block, out, slice(start, None), sem)


def cost(microseconds):
    return pl.CostEstimate(
        flops=int(microseconds * 1_000_000_000), bytes_accessed=0, transcendentals=0
    )


def params(mib):
    return pltpu.CompilerParams(vmem_limit_bytes=mib * 2**20)


def shards(queries, keys, values, out_weight, residual, gate, block_mask):
    rows, width = queries.shape
    columns = out_weight.shape[1]
    seq, tp = lax.axis_size("seq"), lax.axis_size("tp")
    half = seq // 2
    cores = 2
    chips = tp // cores
    share = rows // tp
    part = width // 2
    peers = chips - 1
    cut = columns * CUT_NUM // CUT_DEN // LANES * LANES
    head = (columns - cut) * HEAD_NUM // HEAD_DEN // LANES * LANES

    def swap(array, place):
        return lax.ppermute(array, "seq", [(i, i ^ place) for i in range(seq)])

    def across(array, place, core):
        return lax.ppermute(
            array,
            ("seq", "tp"),
            [
                (i * tp + t, (i ^ place) * tp + (t ^ core))
                for i in range(seq)
                for t in range(tp)
            ],
        )

    def swap_cores(array):
        return lax.ppermute(array, "tp", [(t, t ^ 1) for t in range(tp)])

    def to_chip(array, step):
        return lax.ppermute(
            array,
            "tp",
            [(t, (t // cores + step) % chips * cores + t % cores) for t in range(tp)],
        )

    def in_hbm(*arrays):
        return [pltpu.with_memory_space_constraint(array, pltpu.HBM) for array in arrays]

    kv_keep, kv_send, q_keep, q_send, left = pl.pallas_call(
        functools.partial(pack, half),
        out_shape=[bf16(2 * rows, part)] * 2 + [bf16(rows, part)] * 2 + [bf16(width, cut)],
        in_specs=[pl.BlockSpec(memory_space=pl.ANY)] * 4,
        out_specs=in_vmem(5),
        scratch_shapes=[pltpu.SemaphoreType.DMA((7,))],
        compiler_params=params(16),
        cost_estimate=cost(1.6),
        name="pack",
    )(*in_hbm(queries, keys, values, out_weight))
    kv_far = swap(kv_send, half)
    order = sorted(range(1, half), key=lambda m: (m % 2 == 0, -m))
    direct = [m for m in order if m % 2 == 0 or m == 1]
    near = {m: swap(kv_keep, m) for m in direct}
    chip_weights = [to_chip(left, step) for step in range(1, chips)]
    core_weight = swap_cores(out_weight)
    kv_far, weight, q_send, core_weight = lax.optimization_barrier((kv_far, out_weight, q_send, core_weight))
    q_far = swap(q_send, half)
    far = {m: swap(kv_far, m) for m in order}
    for m in order:
        if m not in direct:
            near[m] = swap(near[m - 1], 1)
    right = pl.pallas_call(
        stage,
        out_shape=bf16(width, columns - cut),
        in_specs=[pl.BlockSpec(memory_space=pl.ANY)],
        out_specs=pl.BlockSpec(memory_space=VMEM),
        scratch_shapes=[pltpu.SemaphoreType.DMA],
        compiler_params=params(16),
        cost_estimate=cost(1.3),
        name="stage",
    )(*in_hbm(weight))
    near[0], far[0] = kv_keep, kv_far
    places = [0] + order
    batches = [places[at : at + BATCH] for at in range(0, len(places), BATCH)]
    blocks = rows // BLOCK
    state_shape = [f32(rows, part)] * 3

    def attend_all(first_row, queries, batches, state, microseconds):
        for at, pieces in enumerate(batches):
            last = at == len(batches) - 1
            out_shape = [bf16(rows // cores, part)] * 2 if last else state_shape
            held = [place for place, _ in pieces]
            state = pl.pallas_call(
                functools.partial(attend_more, first_row, cores, held, last, bool(state)),
                out_shape=out_shape,
                in_specs=in_vmem(2 + len(pieces) + len(state)),
                out_specs=in_vmem(len(out_shape)),
                compiler_params=params(32),
                cost_estimate=cost(microseconds),
                name="attend_far" if first_row else "attend_own",
            )(bias, queries, *[array for _, array in pieces], *state)
        return state

    bias, *own_state = pl.pallas_call(
        functools.partial(attend_first, half, batches[0]),
        out_shape=[f32(2 * blocks * seq * blocks, BLOCK)] + state_shape,
        in_specs=[pl.BlockSpec(memory_space=SMEM)] + in_vmem(1 + len(batches[0])),
        out_specs=in_vmem(4),
        compiler_params=params(32),
        cost_estimate=cost(1.3),
        name="attend_near",
    )(block_mask, q_keep, *[near[m] for m in batches[0]])
    near_batches = [[(m, near[m]) for m in batch] for batch in batches]
    far_batches = [[(m ^ half, far[m]) for m in batch] for batch in batches]
    both = [one + two for one, two in zip(near_batches, far_batches)]
    far_mine, far_other = attend_all(blocks, q_far, both, [], 5)
    own_mine, own_other = attend_all(0, q_keep, near_batches[1:] + far_batches, own_state, 1)
    from_far = across(far_mine, half, 0)
    from_far_core = across(far_other, half, 1)
    from_core = across(own_other, 0, 1)
    lined = pl.pallas_call(
        functools.partial(line_up, half, cores),
        out_shape=[bf16(share, cores * width)] * chips,
        in_specs=in_vmem(4),
        out_specs=in_vmem(chips),
        compiler_params=params(16),
        cost_estimate=cost(0.1),
        name="line_up",
    )(own_mine, from_far_core, from_core, from_far)
    sums = pl.pallas_call(
        functools.partial(project_peers, cut),
        out_shape=[bf16(share, cores * width + head), bf16(share, columns - cut - head)] * peers,
        in_specs=in_vmem(peers + 2),
        out_specs=in_vmem(2 * peers),
        compiler_params=params(32),
        cost_estimate=cost(0.5),
        name="project_peers",
    )(*lined[1:], right, core_weight)
    mine, chip_weights, *_ = lax.optimization_barrier((lined[0], chip_weights, *sums))
    own_left, own_right = pl.pallas_call(
        functools.partial(project_own, cut),
        out_shape=[f32(share, cut), f32(share, columns - cut)],
        in_specs=in_vmem(4),
        out_specs=in_vmem(2),
        compiler_params=params(32),
        cost_estimate=cost(0.1),
        name="project_own",
    )(mine, left, right, core_weight)
    firsts = [to_chip(array, step) for step, array in enumerate(sums[::2], 1)]
    seconds = [to_chip(array, step) for step, array in enumerate(sums[1::2], 1)]
    chip_core_weights = [swap_cores(weight) for weight in chip_weights]
    gate = gate[None, :]
    anywhere = pl.BlockSpec(memory_space=pl.ANY)
    out = pl.pallas_call(
        finish_head,
        out_shape=bf16(share, columns),
        in_specs=in_vmem(3 + peers),
        out_specs=anywhere,
        scratch_shapes=[pltpu.VMEM((share, head), jnp.bfloat16), pltpu.SemaphoreType.DMA],
        compiler_params=params(16),
        cost_estimate=cost(20),
        name="finish_head",
    )(residual, gate, own_right, *firsts)
    out = pl.pallas_call(
        functools.partial(finish_left, peers, cut),
        out_shape=bf16(share, columns),
        in_specs=in_vmem(3 + 3 * peers) + [anywhere],
        out_specs=anywhere,
        scratch_shapes=[pltpu.VMEM((share, cut), jnp.bfloat16), pltpu.SemaphoreType.DMA],
        input_output_aliases={3 + 3 * peers: 0},
        compiler_params=params(32),
        cost_estimate=cost(1.5),
        name="finish_left",
    )(residual, gate, own_left, *firsts, *chip_weights, *chip_core_weights, out)
    return pl.pallas_call(
        finish_right,
        out_shape=bf16(share, columns),
        in_specs=in_vmem(3 + peers) + [pl.BlockSpec(memory_space=pl.ANY)],
        out_specs=pl.BlockSpec(memory_space=pl.ANY),
        scratch_shapes=[
            pltpu.VMEM((share, columns - cut - head), jnp.bfloat16),
            pltpu.SemaphoreType.DMA,
        ],
        input_output_aliases={3 + peers: 0},
        compiler_params=params(16),
        cost_estimate=cost(0.7),
        name="finish_right",
    )(residual, gate, own_right, *seconds, out)


def solution(mesh):
    return jax.shard_map(
        shards,
        mesh=mesh,
        in_specs=(
            P("seq", "tp"),
            P("seq", "tp"),
            P("seq", "tp"),
            P("tp", None),
            P(("seq", "tp"), None),
            P(),
            P(),
        ),
        out_specs=P(("seq", "tp"), None),
        check_vma=False,
    )
```

```python
import functools
import math

import jax
import jax.numpy as jnp
from jax import lax
from jax.experimental import pallas as pl
from jax.experimental.pallas import tpu as pltpu
from jax.sharding import PartitionSpec as P

HD = 128
BLOCK = 128
NEGATIVE = -1e30
LOG2E = math.log2(math.e)
SCORE_SCALE = LOG2E / HD**0.5
BATCH = 4
LANES = 128
CUT_NUM, CUT_DEN = 12, 25
HEAD_NUM, HEAD_DEN = 1, 3

VMEM = pltpu.MemorySpace.VMEM
SMEM = pltpu.MemorySpace.SMEM


def in_vmem(count):
    return [pl.BlockSpec(memory_space=VMEM)] * count


def bf16(*shape):
    return jax.ShapeDtypeStruct(shape, jnp.bfloat16)


def f32(*shape):
    return jax.ShapeDtypeStruct(shape, jnp.float32)


def dot(left, right, contract=((1,), (0,))):
    return lax.dot_general(
        left, right, (contract, ((), ())), preferred_element_type=jnp.float32
    )


def pack(half, q, k, v, weight, kv_keep, kv_send, q_keep, q_send, left, sems):
    rows, width = q.shape
    part = width // 2
    mine = (lax.axis_index("seq") >= half).astype(jnp.int32)
    keep = pl.ds(pl.multiple_of(mine * part, part), part)
    send = pl.ds(pl.multiple_of((1 - mine) * part, part), part)
    copies = [
        (k.at[:, send], kv_send.at[:rows]),
        (v.at[:, send], kv_send.at[rows:]),
        (k.at[:, keep], kv_keep.at[:rows]),
        (v.at[:, keep], kv_keep.at[rows:]),
        (q.at[:, send], q_send),
        (q.at[:, keep], q_keep),
        (weight.at[:, : left.shape[1]], left),
    ]
    copies = [
        pltpu.make_async_copy(source, target, sems.at[n])
        for n, (source, target) in enumerate(copies)
    ]
    for copy in copies:
        copy.start()
    for copy in copies:
        copy.wait()


def attend(queries, first_row, bias, pieces, state):
    rows = queries.shape[0]
    blocks = rows // BLOCK
    outs = {}
    for head in range(queries.shape[1] // HD):
        at = slice(head * HD, (head + 1) * HD)
        raw = [dot(queries[:, at], piece[:rows, at], ((1,), (1,))) for piece, _ in pieces]
        for a in range(blocks):
            band = slice(a * BLOCK, (a + 1) * BLOCK)
            tiles = []
            for n, (_, place) in enumerate(pieces):
                for b in range(blocks):
                    row = (first_row + a) * bias.shape[0] // (2 * blocks) + place * blocks + b
                    tile = raw[n][band, b * BLOCK : (b + 1) * BLOCK]
                    tiles.append(tile * SCORE_SCALE + bias[row : row + 1, :])
            top = jnp.max(functools.reduce(jnp.maximum, tiles), axis=1, keepdims=True)
            if state is not None:
                old_top, old_total, old_summed = (ref[band, at] for ref in state)
                before = old_top[:, :1]
                top = jnp.maximum(top, before)
                fade = jnp.exp2(before - top)
            weights = [jnp.exp2(tile - top) for tile in tiles]
            total = functools.reduce(jnp.add, weights)
            summed = None
            for n, (piece, _) in enumerate(pieces):
                mine = jnp.concatenate(weights[n * blocks : (n + 1) * blocks], axis=1)
                part = dot(mine.astype(jnp.bfloat16), piece[rows:, at])
                summed = part if summed is None else summed + part
            if state is not None:
                total = total + old_total * fade
                summed = summed + old_summed * fade
            outs[head, a] = top, total, summed
    return outs


def keep_state(outs, refs):
    new_top, new_total, new_summed = refs
    for (head, a), (top, total, summed) in outs.items():
        where = (slice(a * BLOCK, (a + 1) * BLOCK), slice(head * HD, (head + 1) * HD))
        new_top[where] = jnp.broadcast_to(top, summed.shape)
        new_total[where] = total
        new_summed[where] = summed


def attend_first(half, places, mask, queries, *refs):
    bias, state = refs[-4], refs[-3:]
    me = lax.axis_index("seq")
    blocks = queries.shape[0] // BLOCK
    keys = bias.shape[0] // (2 * blocks)
    for a in range(2 * blocks):
        row = (me if a < blocks else me ^ half) * blocks + a % blocks
        for b in range(keys):
            column = (me ^ (b // blocks)) * blocks + b % blocks
            allowed = jnp.where(mask[row, column] > 0, 0.0, NEGATIVE)
            bias[a * keys + b : a * keys + b + 1, :] = jnp.full((1, BLOCK), allowed, jnp.float32)
    keep_state(attend(queries, 0, bias, list(zip(refs, places)), None), state)


def attend_more(first_row, cores, places, last, stateful, bias, queries, *refs):
    pieces, rest = list(zip(refs, places)), refs[len(places) :]
    state = None
    if stateful:
        state, rest = rest[:3], rest[3:]
    outs = attend(queries, first_row, bias, pieces, state)
    if not last:
        keep_state(outs, rest)
        return
    mine, other = rest
    core = lax.rem(lax.axis_index("tp"), cores)
    chips = lax.axis_size("tp") // cores
    rows, width = queries.shape
    share = rows // (chips * cores)
    for head in range(width // HD):
        at = slice(head * HD, (head + 1) * HD)
        whole = []
        for a in range(rows // BLOCK):
            _, total, summed = outs[head, a]
            whole.append((summed / jnp.sum(total, axis=1, keepdims=True)).astype(jnp.bfloat16))
        whole = jnp.concatenate(whole, axis=0)
        for chip in range(chips):
            start = chip * cores * share
            one = whole[start : start + share]
            two = whole[start + share : start + 2 * share]
            to = slice(chip * share, (chip + 1) * share)
            mine[to, at] = jnp.where(core == 0, one, two)
            other[to, at] = jnp.where(core == 0, two, one)


def stage(weight, right, sem):
    copy = pltpu.make_async_copy(weight.at[:, weight.shape[1] - right.shape[1] :], right, sem)
    copy.start()
    copy.wait()


def line_up(half, cores, own, far_other, other, far, *outs):
    low = lax.axis_index("seq") < half
    chips = len(outs)
    chip = lax.axis_index("tp") // cores
    share = own.shape[0] // chips
    part = own.shape[1]
    for step, out in enumerate(outs):
        place = lax.rem(chip + step, chips)
        rows = pl.ds(pl.multiple_of(place * share, share), share)
        one, two = own[rows], far[rows]
        out[:, :part] = jnp.where(low, one, two)
        out[:, part : 2 * part] = jnp.where(low, two, one)
        one, two = other[rows], far_other[rows]
        out[:, 2 * part : 3 * part] = jnp.where(low, one, two)
        out[:, 3 * part :] = jnp.where(low, two, one)


def project(attended, weight, core_weight, cut):
    rows = weight.shape[0]
    return dot(attended[:, :rows], weight[...]) + dot(attended[:, rows:], core_weight[:, cut])


def project_heads(cut, *refs):
    peers = (len(refs) - 2) // 2
    right, core_weight = refs[peers : peers + 2]
    for attended, out in zip(refs[:peers], refs[peers + 2 :]):
        rows = attended.shape[1]
        head = out.shape[1] - rows
        out[:, :rows] = attended[...]
        out[:, rows:] = project(
            attended, right.at[:, :head], core_weight, slice(cut, cut + head)
        ).astype(jnp.bfloat16)


def project_tails(*refs):
    peers = (len(refs) - 2) // 2
    right, core_weight = refs[peers : peers + 2]
    for attended, out in zip(refs[:peers], refs[peers + 2 :]):
        start = right.shape[1] - out.shape[1]
        columns = slice(core_weight.shape[1] - out.shape[1], None)
        out[...] = project(attended, right.at[:, start:], core_weight, columns).astype(jnp.bfloat16)


def project_own(cut, attended, left, right, core_weight, out_left, out_right):
    out_left[...] = project(attended, left, core_weight, slice(0, cut))
    out_right[...] = project(attended, right, core_weight, slice(cut, None))


def gated(residual, gate, branch):
    return (residual.astype(jnp.float32) + gate * branch).astype(jnp.bfloat16)


def write_out(block, out, columns, sem):
    copy = pltpu.make_async_copy(block, out.at[:, columns], sem)
    copy.start()
    copy.wait()


def finish_head(residual, gate, own_right, *refs):
    firsts, (out, block, sem) = refs[:-3], refs[-3:]
    head = block.shape[1]
    cut = out.shape[1] - own_right.shape[1]
    branch = own_right[:, :head]
    for first in firsts:
        branch = branch + first[:, first.shape[1] - head :].astype(jnp.float32)
    columns = slice(cut, cut + head)
    block[...] = gated(residual[:, columns], gate[:, columns], branch)
    write_out(block, out, columns, sem)


def finish_left(peers, cut, residual, gate, own, *refs):
    firsts, weights, core_weights = refs[:peers], refs[peers : 2 * peers], refs[2 * peers : 3 * peers]
    _, out, block, sem = refs[3 * peers :]
    branch = own[...]
    for first, weight, core_weight in zip(firsts, weights, core_weights):
        rows = 2 * weight.shape[0]
        branch = branch + project(first.at[:, :rows], weight, core_weight, slice(None))
    block[...] = gated(residual[:, :cut], gate[:, :cut], branch)
    write_out(block, out, slice(0, cut), sem)


def finish_right(residual, gate, own, *refs):
    seconds, (_, out, block, sem) = refs[:-4], refs[-4:]
    tail = block.shape[1]
    start = out.shape[1] - tail
    branch = own[:, own.shape[1] - tail :]
    for second in seconds:
        branch = branch + second[...].astype(jnp.float32)
    block[...] = gated(residual[:, start:], gate[:, start:], branch)
    write_out(block, out, slice(start, None), sem)


def cost(microseconds):
    return pl.CostEstimate(
        flops=int(microseconds * 1_000_000_000), bytes_accessed=0, transcendentals=0
    )


def params(mib):
    return pltpu.CompilerParams(vmem_limit_bytes=mib * 2**20)


def shards(queries, keys, values, out_weight, residual, gate, block_mask):
    rows, width = queries.shape
    columns = out_weight.shape[1]
    seq, tp = lax.axis_size("seq"), lax.axis_size("tp")
    half = seq // 2
    cores = 2
    chips = tp // cores
    share = rows // tp
    part = width // 2
    peers = chips - 1
    cut = columns * CUT_NUM // CUT_DEN // LANES * LANES
    head = (columns - cut) * HEAD_NUM // HEAD_DEN // LANES * LANES

    def swap(array, place):
        return lax.ppermute(array, "seq", [(i, i ^ place) for i in range(seq)])

    def across(array, place, core):
        return lax.ppermute(
            array,
            ("seq", "tp"),
            [
                (i * tp + t, (i ^ place) * tp + (t ^ core))
                for i in range(seq)
                for t in range(tp)
            ],
        )

    def swap_cores(array):
        return lax.ppermute(array, "tp", [(t, t ^ 1) for t in range(tp)])

    def to_chip(array, step):
        return lax.ppermute(
            array,
            "tp",
            [(t, (t // cores + step) % chips * cores + t % cores) for t in range(tp)],
        )

    def in_hbm(*arrays):
        return [pltpu.with_memory_space_constraint(array, pltpu.HBM) for array in arrays]

    kv_keep, kv_send, q_keep, q_send, left = pl.pallas_call(
        functools.partial(pack, half),
        out_shape=[bf16(2 * rows, part)] * 2 + [bf16(rows, part)] * 2 + [bf16(width, cut)],
        in_specs=[pl.BlockSpec(memory_space=pl.ANY)] * 4,
        out_specs=in_vmem(5),
        scratch_shapes=[pltpu.SemaphoreType.DMA((7,))],
        compiler_params=params(16),
        cost_estimate=cost(1.6),
        name="pack",
    )(*in_hbm(queries, keys, values, out_weight))
    kv_far = swap(kv_send, half)
    order = sorted(range(1, half), key=lambda m: (m % 2 == 0, -m))
    direct = [m for m in order if m % 2 == 0 or m == 1]
    near = {m: swap(kv_keep, m) for m in direct}
    chip_weights = [to_chip(left, step) for step in range(1, chips)]
    core_weight = swap_cores(out_weight)
    kv_far, weight, q_send, core_weight = lax.optimization_barrier((kv_far, out_weight, q_send, core_weight))
    q_far = swap(q_send, half)
    far = {m: swap(kv_far, m) for m in order}
    for m in order:
        if m not in direct:
            near[m] = swap(near[m - 1], 1)
    right = pl.pallas_call(
        stage,
        out_shape=bf16(width, columns - cut),
        in_specs=[pl.BlockSpec(memory_space=pl.ANY)],
        out_specs=pl.BlockSpec(memory_space=VMEM),
        scratch_shapes=[pltpu.SemaphoreType.DMA],
        compiler_params=params(16),
        cost_estimate=cost(1.3),
        name="stage",
    )(*in_hbm(weight))
    near[0], far[0] = kv_keep, kv_far
    places = [0] + order
    batches = [places[at : at + BATCH] for at in range(0, len(places), BATCH)]
    blocks = rows // BLOCK
    state_shape = [f32(rows, part)] * 3

    def attend_all(first_row, queries, batches, state, microseconds):
        for at, pieces in enumerate(batches):
            last = at == len(batches) - 1
            out_shape = [bf16(rows // cores, part)] * 2 if last else state_shape
            held = [place for place, _ in pieces]
            state = pl.pallas_call(
                functools.partial(attend_more, first_row, cores, held, last, bool(state)),
                out_shape=out_shape,
                in_specs=in_vmem(2 + len(pieces) + len(state)),
                out_specs=in_vmem(len(out_shape)),
                compiler_params=params(32),
                cost_estimate=cost(microseconds),
                name="attend_far" if first_row else "attend_own",
            )(bias, queries, *[array for _, array in pieces], *state)
        return state

    bias, *own_state = pl.pallas_call(
        functools.partial(attend_first, half, batches[0]),
        out_shape=[f32(2 * blocks * seq * blocks, BLOCK)] + state_shape,
        in_specs=[pl.BlockSpec(memory_space=SMEM)] + in_vmem(1 + len(batches[0])),
        out_specs=in_vmem(4),
        compiler_params=params(32),
        cost_estimate=cost(1.3),
        name="attend_near",
    )(block_mask, q_keep, *[near[m] for m in batches[0]])
    near_batches = [[(m, near[m]) for m in batch] for batch in batches]
    far_batches = [[(m ^ half, far[m]) for m in batch] for batch in batches]
    both = [one + two for one, two in zip(near_batches, far_batches)]
    far_mine, far_other = attend_all(blocks, q_far, both, [], 5)
    own_mine, own_other = attend_all(0, q_keep, near_batches[1:] + far_batches, own_state, 1)
    from_far = across(far_mine, half, 0)
    from_far_core = across(far_other, half, 1)
    from_core = across(own_other, 0, 1)
    lined = pl.pallas_call(
        functools.partial(line_up, half, cores),
        out_shape=[bf16(share, cores * width)] * chips,
        in_specs=in_vmem(4),
        out_specs=in_vmem(chips),
        compiler_params=params(16),
        cost_estimate=cost(0.1),
        name="line_up",
    )(own_mine, from_far_core, from_core, from_far)
    heads = pl.pallas_call(
        functools.partial(project_heads, cut),
        out_shape=[bf16(share, cores * width + head)] * peers,
        in_specs=in_vmem(peers + 2),
        out_specs=in_vmem(peers),
        compiler_params=params(32),
        cost_estimate=cost(0.3),
        name="project_heads",
    )(*lined[1:], right, core_weight)
    tails = pl.pallas_call(
        project_tails,
        out_shape=[bf16(share, columns - cut - head)] * peers,
        in_specs=in_vmem(peers + 2),
        out_specs=in_vmem(peers),
        compiler_params=params(32),
        cost_estimate=cost(0.4),
        name="project_tails",
    )(*lined[1:], right, core_weight)
    sums = [*heads, *tails]
    mine, chip_weights, *_ = lax.optimization_barrier((lined[0], chip_weights, *sums))
    own_left, own_right = pl.pallas_call(
        functools.partial(project_own, cut),
        out_shape=[f32(share, cut), f32(share, columns - cut)],
        in_specs=in_vmem(4),
        out_specs=in_vmem(2),
        compiler_params=params(32),
        cost_estimate=cost(0.1),
        name="project_own",
    )(mine, left, right, core_weight)
    firsts = [to_chip(array, step) for step, array in enumerate(heads, 1)]
    seconds = [to_chip(array, step) for step, array in enumerate(tails, 1)]
    chip_core_weights = [swap_cores(weight) for weight in chip_weights]
    gate = gate[None, :]
    anywhere = pl.BlockSpec(memory_space=pl.ANY)
    out = pl.pallas_call(
        finish_head,
        out_shape=bf16(share, columns),
        in_specs=in_vmem(3 + peers),
        out_specs=anywhere,
        scratch_shapes=[pltpu.VMEM((share, head), jnp.bfloat16), pltpu.SemaphoreType.DMA],
        compiler_params=params(16),
        cost_estimate=cost(20),
        name="finish_head",
    )(residual, gate, own_right, *firsts)
    out = pl.pallas_call(
        functools.partial(finish_left, peers, cut),
        out_shape=bf16(share, columns),
        in_specs=in_vmem(3 + 3 * peers) + [anywhere],
        out_specs=anywhere,
        scratch_shapes=[pltpu.VMEM((share, cut), jnp.bfloat16), pltpu.SemaphoreType.DMA],
        input_output_aliases={3 + 3 * peers: 0},
        compiler_params=params(32),
        cost_estimate=cost(1.5),
        name="finish_left",
    )(residual, gate, own_left, *firsts, *chip_weights, *chip_core_weights, out)
    return pl.pallas_call(
        finish_right,
        out_shape=bf16(share, columns),
        in_specs=in_vmem(3 + peers) + [pl.BlockSpec(memory_space=pl.ANY)],
        out_specs=pl.BlockSpec(memory_space=pl.ANY),
        scratch_shapes=[
            pltpu.VMEM((share, columns - cut - head), jnp.bfloat16),
            pltpu.SemaphoreType.DMA,
        ],
        input_output_aliases={3 + peers: 0},
        compiler_params=params(16),
        cost_estimate=cost(0.7),
        name="finish_right",
    )(residual, gate, own_right, *seconds, out)


def solution(mesh):
    return jax.shard_map(
        shards,
        mesh=mesh,
        in_specs=(
            P("seq", "tp"),
            P("seq", "tp"),
            P("seq", "tp"),
            P("tp", None),
            P(("seq", "tp"), None),
            P(),
            P(),
        ),
        out_specs=P(("seq", "tp"), None),
        check_vma=False,
    )
```

```python
import functools
import math

import jax
import jax.numpy as jnp
from jax import lax
from jax.experimental import pallas as pl
from jax.experimental.pallas import tpu as pltpu
from jax.sharding import PartitionSpec as P

HD = 128
BLOCK = 128
NEGATIVE = -1e30
LOG2E = math.log2(math.e)
SCORE_SCALE = LOG2E / HD**0.5
BATCH = 4
LANES = 128
CUT_NUM, CUT_DEN = 12, 25
HEAD_NUM, HEAD_DEN = 9, 20

VMEM = pltpu.MemorySpace.VMEM
SMEM = pltpu.MemorySpace.SMEM


def in_vmem(count):
    return [pl.BlockSpec(memory_space=VMEM)] * count


def bf16(*shape):
    return jax.ShapeDtypeStruct(shape, jnp.bfloat16)


def f32(*shape):
    return jax.ShapeDtypeStruct(shape, jnp.float32)


def dot(left, right, contract=((1,), (0,))):
    return lax.dot_general(
        left, right, (contract, ((), ())), preferred_element_type=jnp.float32
    )


def pack(half, q, k, v, weight, kv_keep, kv_send, q_keep, q_send, left, sems):
    rows, width = q.shape
    part = width // 2
    mine = (lax.axis_index("seq") >= half).astype(jnp.int32)
    keep = pl.ds(pl.multiple_of(mine * part, part), part)
    send = pl.ds(pl.multiple_of((1 - mine) * part, part), part)
    copies = [
        (k.at[:, send], kv_send.at[:rows]),
        (v.at[:, send], kv_send.at[rows:]),
        (k.at[:, keep], kv_keep.at[:rows]),
        (v.at[:, keep], kv_keep.at[rows:]),
        (q.at[:, send], q_send),
        (q.at[:, keep], q_keep),
        (weight.at[:, : left.shape[1]], left),
    ]
    copies = [
        pltpu.make_async_copy(source, target, sems.at[n])
        for n, (source, target) in enumerate(copies)
    ]
    for copy in copies:
        copy.start()
    for copy in copies:
        copy.wait()


def attend(queries, first_row, bias, pieces, state):
    rows = queries.shape[0]
    blocks = rows // BLOCK
    outs = {}
    for head in range(queries.shape[1] // HD):
        at = slice(head * HD, (head + 1) * HD)
        raw = [dot(queries[:, at], piece[:rows, at], ((1,), (1,))) for piece, _ in pieces]
        for a in range(blocks):
            band = slice(a * BLOCK, (a + 1) * BLOCK)
            tiles = []
            for n, (_, place) in enumerate(pieces):
                for b in range(blocks):
                    row = (first_row + a) * bias.shape[0] // (2 * blocks) + place * blocks + b
                    tile = raw[n][band, b * BLOCK : (b + 1) * BLOCK]
                    tiles.append(tile * SCORE_SCALE + bias[row : row + 1, :])
            top = jnp.max(functools.reduce(jnp.maximum, tiles), axis=1, keepdims=True)
            if state is not None:
                old_top, old_total, old_summed = (ref[band, at] for ref in state)
                before = old_top[:, :1]
                top = jnp.maximum(top, before)
                fade = jnp.exp2(before - top)
            weights = [jnp.exp2(tile - top) for tile in tiles]
            total = functools.reduce(jnp.add, weights)
            summed = None
            for n, (piece, _) in enumerate(pieces):
                mine = jnp.concatenate(weights[n * blocks : (n + 1) * blocks], axis=1)
                part = dot(mine.astype(jnp.bfloat16), piece[rows:, at])
                summed = part if summed is None else summed + part
            if state is not None:
                total = total + old_total * fade
                summed = summed + old_summed * fade
            outs[head, a] = top, total, summed
    return outs


def keep_state(outs, refs):
    new_top, new_total, new_summed = refs
    for (head, a), (top, total, summed) in outs.items():
        where = (slice(a * BLOCK, (a + 1) * BLOCK), slice(head * HD, (head + 1) * HD))
        new_top[where] = jnp.broadcast_to(top, summed.shape)
        new_total[where] = total
        new_summed[where] = summed


def attend_first(half, places, mask, queries, *refs):
    bias, state = refs[-4], refs[-3:]
    me = lax.axis_index("seq")
    blocks = queries.shape[0] // BLOCK
    keys = bias.shape[0] // (2 * blocks)
    for a in range(2 * blocks):
        row = (me if a < blocks else me ^ half) * blocks + a % blocks
        for b in range(keys):
            column = (me ^ (b // blocks)) * blocks + b % blocks
            allowed = jnp.where(mask[row, column] > 0, 0.0, NEGATIVE)
            bias[a * keys + b : a * keys + b + 1, :] = jnp.full((1, BLOCK), allowed, jnp.float32)
    keep_state(attend(queries, 0, bias, list(zip(refs, places)), None), state)


def attend_more(first_row, cores, places, last, stateful, bias, queries, *refs):
    pieces, rest = list(zip(refs, places)), refs[len(places) :]
    state = None
    if stateful:
        state, rest = rest[:3], rest[3:]
    outs = attend(queries, first_row, bias, pieces, state)
    if not last:
        keep_state(outs, rest)
        return
    mine, other = rest
    core = lax.rem(lax.axis_index("tp"), cores)
    chips = lax.axis_size("tp") // cores
    rows, width = queries.shape
    share = rows // (chips * cores)
    for head in range(width // HD):
        at = slice(head * HD, (head + 1) * HD)
        whole = []
        for a in range(rows // BLOCK):
            _, total, summed = outs[head, a]
            whole.append((summed / jnp.sum(total, axis=1, keepdims=True)).astype(jnp.bfloat16))
        whole = jnp.concatenate(whole, axis=0)
        for chip in range(chips):
            start = chip * cores * share
            one = whole[start : start + share]
            two = whole[start + share : start + 2 * share]
            to = slice(chip * share, (chip + 1) * share)
            mine[to, at] = jnp.where(core == 0, one, two)
            other[to, at] = jnp.where(core == 0, two, one)


def stage(weight, right, sem):
    copy = pltpu.make_async_copy(weight.at[:, weight.shape[1] - right.shape[1] :], right, sem)
    copy.start()
    copy.wait()


def line_up(half, cores, own, far_other, other, far, *outs):
    low = lax.axis_index("seq") < half
    chips = len(outs)
    chip = lax.axis_index("tp") // cores
    share = own.shape[0] // chips
    part = own.shape[1]
    for step, out in enumerate(outs):
        place = lax.rem(chip + step, chips)
        rows = pl.ds(pl.multiple_of(place * share, share), share)
        one, two = own[rows], far[rows]
        out[:, :part] = jnp.where(low, one, two)
        out[:, part : 2 * part] = jnp.where(low, two, one)
        one, two = other[rows], far_other[rows]
        out[:, 2 * part : 3 * part] = jnp.where(low, one, two)
        out[:, 3 * part :] = jnp.where(low, two, one)


def project(attended, weight, core_weight, cut):
    rows = weight.shape[0]
    return dot(attended[:, :rows], weight[...]) + dot(attended[:, rows:], core_weight[:, cut])


def project_heads(cut, *refs):
    peers = (len(refs) - 2) // 2
    right, core_weight = refs[peers : peers + 2]
    for attended, out in zip(refs[:peers], refs[peers + 2 :]):
        rows = attended.shape[1]
        head = out.shape[1] - rows
        out[:, :rows] = attended[...]
        out[:, rows:] = project(
            attended, right.at[:, :head], core_weight, slice(cut, cut + head)
        ).astype(jnp.bfloat16)


def project_tails(*refs):
    peers = (len(refs) - 2) // 2
    right, core_weight = refs[peers : peers + 2]
    for attended, out in zip(refs[:peers], refs[peers + 2 :]):
        start = right.shape[1] - out.shape[1]
        columns = slice(core_weight.shape[1] - out.shape[1], None)
        out[...] = project(attended, right.at[:, start:], core_weight, columns).astype(jnp.bfloat16)


def project_own(cut, attended, left, right, core_weight, out_left, out_right):
    out_left[...] = project(attended, left, core_weight, slice(0, cut))
    out_right[...] = project(attended, right, core_weight, slice(cut, None))


def gated(residual, gate, branch):
    return (residual.astype(jnp.float32) + gate * branch).astype(jnp.bfloat16)


def write_out(block, out, columns, sem):
    copy = pltpu.make_async_copy(block, out.at[:, columns], sem)
    copy.start()
    copy.wait()


def finish_head(residual, gate, own_right, *refs):
    firsts, (out, block, sem) = refs[:-3], refs[-3:]
    head = block.shape[1]
    cut = out.shape[1] - own_right.shape[1]
    branch = own_right[:, :head]
    for first in firsts:
        branch = branch + first[:, first.shape[1] - head :].astype(jnp.float32)
    columns = slice(cut, cut + head)
    block[...] = gated(residual[:, columns], gate[:, columns], branch)
    write_out(block, out, columns, sem)


def finish_left(peers, cut, residual, gate, own, *refs):
    firsts, weights, core_weights = refs[:peers], refs[peers : 2 * peers], refs[2 * peers : 3 * peers]
    _, out, block, sem = refs[3 * peers :]
    branch = own[...]
    for first, weight, core_weight in zip(firsts, weights, core_weights):
        rows = 2 * weight.shape[0]
        branch = branch + project(first.at[:, :rows], weight, core_weight, slice(None))
    block[...] = gated(residual[:, :cut], gate[:, :cut], branch)
    write_out(block, out, slice(0, cut), sem)


def finish_right(residual, gate, own, *refs):
    seconds, (_, out, block, sem) = refs[:-4], refs[-4:]
    tail = block.shape[1]
    start = out.shape[1] - tail
    branch = own[:, own.shape[1] - tail :]
    for second in seconds:
        branch = branch + second[...].astype(jnp.float32)
    block[...] = gated(residual[:, start:], gate[:, start:], branch)
    write_out(block, out, slice(start, None), sem)


def cost(microseconds):
    return pl.CostEstimate(
        flops=int(microseconds * 1_000_000_000), bytes_accessed=0, transcendentals=0
    )


def params(mib):
    return pltpu.CompilerParams(vmem_limit_bytes=mib * 2**20)


def shards(queries, keys, values, out_weight, residual, gate, block_mask):
    rows, width = queries.shape
    columns = out_weight.shape[1]
    seq, tp = lax.axis_size("seq"), lax.axis_size("tp")
    half = seq // 2
    cores = 2
    chips = tp // cores
    share = rows // tp
    part = width // 2
    peers = chips - 1
    cut = columns * CUT_NUM // CUT_DEN // LANES * LANES
    head = (columns - cut) * HEAD_NUM // HEAD_DEN // LANES * LANES

    def swap(array, place):
        return lax.ppermute(array, "seq", [(i, i ^ place) for i in range(seq)])

    def across(array, place, core):
        return lax.ppermute(
            array,
            ("seq", "tp"),
            [
                (i * tp + t, (i ^ place) * tp + (t ^ core))
                for i in range(seq)
                for t in range(tp)
            ],
        )

    def swap_cores(array):
        return lax.ppermute(array, "tp", [(t, t ^ 1) for t in range(tp)])

    def to_chip(array, step):
        return lax.ppermute(
            array,
            "tp",
            [(t, (t // cores + step) % chips * cores + t % cores) for t in range(tp)],
        )

    def in_hbm(*arrays):
        return [pltpu.with_memory_space_constraint(array, pltpu.HBM) for array in arrays]

    kv_keep, kv_send, q_keep, q_send, left = pl.pallas_call(
        functools.partial(pack, half),
        out_shape=[bf16(2 * rows, part)] * 2 + [bf16(rows, part)] * 2 + [bf16(width, cut)],
        in_specs=[pl.BlockSpec(memory_space=pl.ANY)] * 4,
        out_specs=in_vmem(5),
        scratch_shapes=[pltpu.SemaphoreType.DMA((7,))],
        compiler_params=params(16),
        cost_estimate=cost(1.6),
        name="pack",
    )(*in_hbm(queries, keys, values, out_weight))
    kv_far = swap(kv_send, half)
    order = sorted(range(1, half), key=lambda m: (m % 2 == 0, -m))
    direct = [m for m in order if m % 2 == 0 or m == 1]
    near = {m: swap(kv_keep, m) for m in direct}
    chip_weights = [to_chip(left, step) for step in range(1, chips)]
    core_weight = swap_cores(out_weight)
    kv_far, weight, q_send, core_weight = lax.optimization_barrier((kv_far, out_weight, q_send, core_weight))
    q_far = swap(q_send, half)
    far = {m: swap(kv_far, m) for m in order}
    for m in order:
        if m not in direct:
            near[m] = swap(near[m - 1], 1)
    right = pl.pallas_call(
        stage,
        out_shape=bf16(width, columns - cut),
        in_specs=[pl.BlockSpec(memory_space=pl.ANY)],
        out_specs=pl.BlockSpec(memory_space=VMEM),
        scratch_shapes=[pltpu.SemaphoreType.DMA],
        compiler_params=params(16),
        cost_estimate=cost(1.3),
        name="stage",
    )(*in_hbm(weight))
    near[0], far[0] = kv_keep, kv_far
    places = [0] + order
    batches = [places[at : at + BATCH] for at in range(0, len(places), BATCH)]
    blocks = rows // BLOCK
    state_shape = [f32(rows, part)] * 3

    def attend_all(first_row, queries, batches, state, microseconds):
        for at, pieces in enumerate(batches):
            last = at == len(batches) - 1
            out_shape = [bf16(rows // cores, part)] * 2 if last else state_shape
            held = [place for place, _ in pieces]
            state = pl.pallas_call(
                functools.partial(attend_more, first_row, cores, held, last, bool(state)),
                out_shape=out_shape,
                in_specs=in_vmem(2 + len(pieces) + len(state)),
                out_specs=in_vmem(len(out_shape)),
                compiler_params=params(32),
                cost_estimate=cost(microseconds),
                name="attend_far" if first_row else "attend_own",
            )(bias, queries, *[array for _, array in pieces], *state)
        return state

    bias, *own_state = pl.pallas_call(
        functools.partial(attend_first, half, batches[0]),
        out_shape=[f32(2 * blocks * seq * blocks, BLOCK)] + state_shape,
        in_specs=[pl.BlockSpec(memory_space=SMEM)] + in_vmem(1 + len(batches[0])),
        out_specs=in_vmem(4),
        compiler_params=params(32),
        cost_estimate=cost(1.3),
        name="attend_near",
    )(block_mask, q_keep, *[near[m] for m in batches[0]])
    near_batches = [[(m, near[m]) for m in batch] for batch in batches]
    far_batches = [[(m ^ half, far[m]) for m in batch] for batch in batches]
    both = [one + two for one, two in zip(near_batches, far_batches)]
    far_mine, far_other = attend_all(blocks, q_far, both, [], 5)
    own_mine, own_other = attend_all(0, q_keep, near_batches[1:] + far_batches, own_state, 1)
    from_far = across(far_mine, half, 0)
    from_far_core = across(far_other, half, 1)
    from_core = across(own_other, 0, 1)
    lined = pl.pallas_call(
        functools.partial(line_up, half, cores),
        out_shape=[bf16(share, cores * width)] * chips,
        in_specs=in_vmem(4),
        out_specs=in_vmem(chips),
        compiler_params=params(16),
        cost_estimate=cost(0.1),
        name="line_up",
    )(own_mine, from_far_core, from_core, from_far)
    heads = pl.pallas_call(
        functools.partial(project_heads, cut),
        out_shape=[bf16(share, cores * width + head)] * peers,
        in_specs=in_vmem(peers + 2),
        out_specs=in_vmem(peers),
        compiler_params=params(32),
        cost_estimate=cost(0.3),
        name="project_heads",
    )(*lined[1:], right, core_weight)
    tails = pl.pallas_call(
        project_tails,
        out_shape=[bf16(share, columns - cut - head)] * peers,
        in_specs=in_vmem(peers + 2),
        out_specs=in_vmem(peers),
        compiler_params=params(32),
        cost_estimate=cost(0.4),
        name="project_tails",
    )(*lined[1:], right, core_weight)
    sums = [*heads, *tails]
    mine, chip_weights, *_ = lax.optimization_barrier((lined[0], chip_weights, *sums))
    own_left, own_right = pl.pallas_call(
        functools.partial(project_own, cut),
        out_shape=[f32(share, cut), f32(share, columns - cut)],
        in_specs=in_vmem(4),
        out_specs=in_vmem(2),
        compiler_params=params(32),
        cost_estimate=cost(0.1),
        name="project_own",
    )(mine, left, right, core_weight)
    firsts = [to_chip(array, step) for step, array in enumerate(heads, 1)]
    seconds = [to_chip(array, step) for step, array in enumerate(tails, 1)]
    chip_core_weights = [swap_cores(weight) for weight in chip_weights]
    gate = gate[None, :]
    anywhere = pl.BlockSpec(memory_space=pl.ANY)
    out = pl.pallas_call(
        finish_head,
        out_shape=bf16(share, columns),
        in_specs=in_vmem(3 + peers),
        out_specs=anywhere,
        scratch_shapes=[pltpu.VMEM((share, head), jnp.bfloat16), pltpu.SemaphoreType.DMA],
        compiler_params=params(16),
        cost_estimate=cost(20),
        name="finish_head",
    )(residual, gate, own_right, *firsts)
    out = pl.pallas_call(
        functools.partial(finish_left, peers, cut),
        out_shape=bf16(share, columns),
        in_specs=in_vmem(3 + 3 * peers) + [anywhere],
        out_specs=anywhere,
        scratch_shapes=[pltpu.VMEM((share, cut), jnp.bfloat16), pltpu.SemaphoreType.DMA],
        input_output_aliases={3 + 3 * peers: 0},
        compiler_params=params(32),
        cost_estimate=cost(1.5),
        name="finish_left",
    )(residual, gate, own_left, *firsts, *chip_weights, *chip_core_weights, out)
    return pl.pallas_call(
        finish_right,
        out_shape=bf16(share, columns),
        in_specs=in_vmem(3 + peers) + [pl.BlockSpec(memory_space=pl.ANY)],
        out_specs=pl.BlockSpec(memory_space=pl.ANY),
        scratch_shapes=[
            pltpu.VMEM((share, columns - cut - head), jnp.bfloat16),
            pltpu.SemaphoreType.DMA,
        ],
        input_output_aliases={3 + peers: 0},
        compiler_params=params(16),
        cost_estimate=cost(0.7),
        name="finish_right",
    )(residual, gate, own_right, *seconds, out)


def solution(mesh):
    return jax.shard_map(
        shards,
        mesh=mesh,
        in_specs=(
            P("seq", "tp"),
            P("seq", "tp"),
            P("seq", "tp"),
            P("tp", None),
            P(("seq", "tp"), None),
            P(),
            P(),
        ),
        out_specs=P(("seq", "tp"), None),
        check_vma=False,
    )
```

```python
import functools
import math

import jax
import jax.numpy as jnp
from jax import lax
from jax.experimental import pallas as pl
from jax.experimental.pallas import tpu as pltpu
from jax.sharding import PartitionSpec as P

HD = 128
BLOCK = 128
NEGATIVE = -1e30
LOG2E = math.log2(math.e)
SCORE_SCALE = LOG2E / HD**0.5
BATCH = 4
LANES = 128
CUT_NUM, CUT_DEN = 23, 50
HEAD_NUM, HEAD_DEN = 9, 20

VMEM = pltpu.MemorySpace.VMEM
SMEM = pltpu.MemorySpace.SMEM


def in_vmem(count):
    return [pl.BlockSpec(memory_space=VMEM)] * count


def bf16(*shape):
    return jax.ShapeDtypeStruct(shape, jnp.bfloat16)


def f32(*shape):
    return jax.ShapeDtypeStruct(shape, jnp.float32)


def dot(left, right, contract=((1,), (0,))):
    return lax.dot_general(
        left, right, (contract, ((), ())), preferred_element_type=jnp.float32
    )


def pack(half, q, k, v, weight, kv_keep, kv_send, q_keep, q_send, left, sems):
    rows, width = q.shape
    part = width // 2
    mine = (lax.axis_index("seq") >= half).astype(jnp.int32)
    keep = pl.ds(pl.multiple_of(mine * part, part), part)
    send = pl.ds(pl.multiple_of((1 - mine) * part, part), part)
    copies = [
        (k.at[:, send], kv_send.at[:rows]),
        (v.at[:, send], kv_send.at[rows:]),
        (k.at[:, keep], kv_keep.at[:rows]),
        (v.at[:, keep], kv_keep.at[rows:]),
        (q.at[:, send], q_send),
        (q.at[:, keep], q_keep),
        (weight.at[:, : left.shape[1]], left),
    ]
    copies = [
        pltpu.make_async_copy(source, target, sems.at[n])
        for n, (source, target) in enumerate(copies)
    ]
    for copy in copies:
        copy.start()
    for copy in copies:
        copy.wait()


def attend(queries, first_row, bias, pieces, state):
    rows = queries.shape[0]
    blocks = rows // BLOCK
    outs = {}
    for head in range(queries.shape[1] // HD):
        at = slice(head * HD, (head + 1) * HD)
        raw = [dot(queries[:, at], piece[:rows, at], ((1,), (1,))) for piece, _ in pieces]
        for a in range(blocks):
            band = slice(a * BLOCK, (a + 1) * BLOCK)
            tiles = []
            for n, (_, place) in enumerate(pieces):
                for b in range(blocks):
                    row = (first_row + a) * bias.shape[0] // (2 * blocks) + place * blocks + b
                    tile = raw[n][band, b * BLOCK : (b + 1) * BLOCK]
                    tiles.append(tile * SCORE_SCALE + bias[row : row + 1, :])
            top = jnp.max(functools.reduce(jnp.maximum, tiles), axis=1, keepdims=True)
            if state is not None:
                old_top, old_total, old_summed = (ref[band, at] for ref in state)
                before = old_top[:, :1]
                top = jnp.maximum(top, before)
                fade = jnp.exp2(before - top)
            weights = [jnp.exp2(tile - top) for tile in tiles]
            total = functools.reduce(jnp.add, weights)
            summed = None
            for n, (piece, _) in enumerate(pieces):
                mine = jnp.concatenate(weights[n * blocks : (n + 1) * blocks], axis=1)
                part = dot(mine.astype(jnp.bfloat16), piece[rows:, at])
                summed = part if summed is None else summed + part
            if state is not None:
                total = total + old_total * fade
                summed = summed + old_summed * fade
            outs[head, a] = top, total, summed
    return outs


def keep_state(outs, refs):
    new_top, new_total, new_summed = refs
    for (head, a), (top, total, summed) in outs.items():
        where = (slice(a * BLOCK, (a + 1) * BLOCK), slice(head * HD, (head + 1) * HD))
        new_top[where] = jnp.broadcast_to(top, summed.shape)
        new_total[where] = total
        new_summed[where] = summed


def attend_first(half, places, mask, queries, *refs):
    bias, state = refs[-4], refs[-3:]
    me = lax.axis_index("seq")
    blocks = queries.shape[0] // BLOCK
    keys = bias.shape[0] // (2 * blocks)
    for a in range(2 * blocks):
        row = (me if a < blocks else me ^ half) * blocks + a % blocks
        for b in range(keys):
            column = (me ^ (b // blocks)) * blocks + b % blocks
            allowed = jnp.where(mask[row, column] > 0, 0.0, NEGATIVE)
            bias[a * keys + b : a * keys + b + 1, :] = jnp.full((1, BLOCK), allowed, jnp.float32)
    keep_state(attend(queries, 0, bias, list(zip(refs, places)), None), state)


def attend_more(first_row, cores, places, last, stateful, bias, queries, *refs):
    pieces, rest = list(zip(refs, places)), refs[len(places) :]
    state = None
    if stateful:
        state, rest = rest[:3], rest[3:]
    outs = attend(queries, first_row, bias, pieces, state)
    if not last:
        keep_state(outs, rest)
        return
    mine, other = rest
    core = lax.rem(lax.axis_index("tp"), cores)
    chips = lax.axis_size("tp") // cores
    rows, width = queries.shape
    share = rows // (chips * cores)
    for head in range(width // HD):
        at = slice(head * HD, (head + 1) * HD)
        whole = []
        for a in range(rows // BLOCK):
            _, total, summed = outs[head, a]
            whole.append((summed / jnp.sum(total, axis=1, keepdims=True)).astype(jnp.bfloat16))
        whole = jnp.concatenate(whole, axis=0)
        for chip in range(chips):
            start = chip * cores * share
            one = whole[start : start + share]
            two = whole[start + share : start + 2 * share]
            to = slice(chip * share, (chip + 1) * share)
            mine[to, at] = jnp.where(core == 0, one, two)
            other[to, at] = jnp.where(core == 0, two, one)


def stage(weight, right, sem):
    copy = pltpu.make_async_copy(weight.at[:, weight.shape[1] - right.shape[1] :], right, sem)
    copy.start()
    copy.wait()


def line_up(half, cores, own, far_other, other, far, *outs):
    low = lax.axis_index("seq") < half
    chips = len(outs)
    chip = lax.axis_index("tp") // cores
    share = own.shape[0] // chips
    part = own.shape[1]
    for step, out in enumerate(outs):
        place = lax.rem(chip + step, chips)
        rows = pl.ds(pl.multiple_of(place * share, share), share)
        one, two = own[rows], far[rows]
        out[:, :part] = jnp.where(low, one, two)
        out[:, part : 2 * part] = jnp.where(low, two, one)
        one, two = other[rows], far_other[rows]
        out[:, 2 * part : 3 * part] = jnp.where(low, one, two)
        out[:, 3 * part :] = jnp.where(low, two, one)


def project(attended, weight, core_weight, cut):
    rows = weight.shape[0]
    return dot(attended[:, :rows], weight[...]) + dot(attended[:, rows:], core_weight[:, cut])


def project_heads(cut, *refs):
    peers = (len(refs) - 2) // 2
    right, core_weight = refs[peers : peers + 2]
    for attended, out in zip(refs[:peers], refs[peers + 2 :]):
        rows = attended.shape[1]
        head = out.shape[1] - rows
        out[:, :rows] = attended[...]
        out[:, rows:] = project(
            attended, right.at[:, :head], core_weight, slice(cut, cut + head)
        ).astype(jnp.bfloat16)


def project_tails(*refs):
    peers = (len(refs) - 2) // 2
    right, core_weight = refs[peers : peers + 2]
    for attended, out in zip(refs[:peers], refs[peers + 2 :]):
        start = right.shape[1] - out.shape[1]
        columns = slice(core_weight.shape[1] - out.shape[1], None)
        out[...] = project(attended, right.at[:, start:], core_weight, columns).astype(jnp.bfloat16)


def project_own(cut, attended, left, right, core_weight, out_left, out_right):
    out_left[...] = project(attended, left, core_weight, slice(0, cut))
    out_right[...] = project(attended, right, core_weight, slice(cut, None))


def gated(residual, gate, branch):
    return (residual.astype(jnp.float32) + gate * branch).astype(jnp.bfloat16)


def write_out(block, out, columns, sem):
    copy = pltpu.make_async_copy(block, out.at[:, columns], sem)
    copy.start()
    copy.wait()


def finish_head(residual, gate, own_right, *refs):
    firsts, (out, block, sem) = refs[:-3], refs[-3:]
    head = block.shape[1]
    cut = out.shape[1] - own_right.shape[1]
    branch = own_right[:, :head]
    for first in firsts:
        branch = branch + first[:, first.shape[1] - head :].astype(jnp.float32)
    columns = slice(cut, cut + head)
    block[...] = gated(residual[:, columns], gate[:, columns], branch)
    write_out(block, out, columns, sem)


def finish_left(peers, cut, residual, gate, own, *refs):
    firsts, weights, core_weights = refs[:peers], refs[peers : 2 * peers], refs[2 * peers : 3 * peers]
    _, out, block, sem = refs[3 * peers :]
    branch = own[...]
    for first, weight, core_weight in zip(firsts, weights, core_weights):
        rows = 2 * weight.shape[0]
        branch = branch + project(first.at[:, :rows], weight, core_weight, slice(None))
    block[...] = gated(residual[:, :cut], gate[:, :cut], branch)
    write_out(block, out, slice(0, cut), sem)


def finish_right(residual, gate, own, *refs):
    seconds, (_, out, block, sem) = refs[:-4], refs[-4:]
    tail = block.shape[1]
    start = out.shape[1] - tail
    branch = own[:, own.shape[1] - tail :]
    for second in seconds:
        branch = branch + second[...].astype(jnp.float32)
    block[...] = gated(residual[:, start:], gate[:, start:], branch)
    write_out(block, out, slice(start, None), sem)


def cost(microseconds):
    return pl.CostEstimate(
        flops=int(microseconds * 1_000_000_000), bytes_accessed=0, transcendentals=0
    )


def params(mib):
    return pltpu.CompilerParams(vmem_limit_bytes=mib * 2**20)


def shards(queries, keys, values, out_weight, residual, gate, block_mask):
    rows, width = queries.shape
    columns = out_weight.shape[1]
    seq, tp = lax.axis_size("seq"), lax.axis_size("tp")
    half = seq // 2
    cores = 2
    chips = tp // cores
    share = rows // tp
    part = width // 2
    peers = chips - 1
    cut = columns * CUT_NUM // CUT_DEN // LANES * LANES
    head = (columns - cut) * HEAD_NUM // HEAD_DEN // LANES * LANES

    def swap(array, place):
        return lax.ppermute(array, "seq", [(i, i ^ place) for i in range(seq)])

    def across(array, place, core):
        return lax.ppermute(
            array,
            ("seq", "tp"),
            [
                (i * tp + t, (i ^ place) * tp + (t ^ core))
                for i in range(seq)
                for t in range(tp)
            ],
        )

    def swap_cores(array):
        return lax.ppermute(array, "tp", [(t, t ^ 1) for t in range(tp)])

    def to_chip(array, step):
        return lax.ppermute(
            array,
            "tp",
            [(t, (t // cores + step) % chips * cores + t % cores) for t in range(tp)],
        )

    def in_hbm(*arrays):
        return [pltpu.with_memory_space_constraint(array, pltpu.HBM) for array in arrays]

    kv_keep, kv_send, q_keep, q_send, left = pl.pallas_call(
        functools.partial(pack, half),
        out_shape=[bf16(2 * rows, part)] * 2 + [bf16(rows, part)] * 2 + [bf16(width, cut)],
        in_specs=[pl.BlockSpec(memory_space=pl.ANY)] * 4,
        out_specs=in_vmem(5),
        scratch_shapes=[pltpu.SemaphoreType.DMA((7,))],
        compiler_params=params(16),
        cost_estimate=cost(1.6),
        name="pack",
    )(*in_hbm(queries, keys, values, out_weight))
    kv_far = swap(kv_send, half)
    order = sorted(range(1, half), key=lambda m: (m % 2 == 0, -m))
    direct = [m for m in order if m % 2 == 0 or m == 1]
    near = {m: swap(kv_keep, m) for m in direct}
    chip_weights = [to_chip(left, step) for step in range(1, chips)]
    core_weight = swap_cores(out_weight)
    kv_far, weight, q_send, core_weight = lax.optimization_barrier((kv_far, out_weight, q_send, core_weight))
    q_far = swap(q_send, half)
    far = {m: swap(kv_far, m) for m in order}
    for m in order:
        if m not in direct:
            near[m] = swap(near[m - 1], 1)
    right = pl.pallas_call(
        stage,
        out_shape=bf16(width, columns - cut),
        in_specs=[pl.BlockSpec(memory_space=pl.ANY)],
        out_specs=pl.BlockSpec(memory_space=VMEM),
        scratch_shapes=[pltpu.SemaphoreType.DMA],
        compiler_params=params(16),
        cost_estimate=cost(1.3),
        name="stage",
    )(*in_hbm(weight))
    near[0], far[0] = kv_keep, kv_far
    places = [0] + order
    batches = [places[at : at + BATCH] for at in range(0, len(places), BATCH)]
    blocks = rows // BLOCK
    state_shape = [f32(rows, part)] * 3

    def attend_all(first_row, queries, batches, state, microseconds):
        for at, pieces in enumerate(batches):
            last = at == len(batches) - 1
            out_shape = [bf16(rows // cores, part)] * 2 if last else state_shape
            held = [place for place, _ in pieces]
            state = pl.pallas_call(
                functools.partial(attend_more, first_row, cores, held, last, bool(state)),
                out_shape=out_shape,
                in_specs=in_vmem(2 + len(pieces) + len(state)),
                out_specs=in_vmem(len(out_shape)),
                compiler_params=params(32),
                cost_estimate=cost(microseconds),
                name="attend_far" if first_row else "attend_own",
            )(bias, queries, *[array for _, array in pieces], *state)
        return state

    bias, *own_state = pl.pallas_call(
        functools.partial(attend_first, half, batches[0]),
        out_shape=[f32(2 * blocks * seq * blocks, BLOCK)] + state_shape,
        in_specs=[pl.BlockSpec(memory_space=SMEM)] + in_vmem(1 + len(batches[0])),
        out_specs=in_vmem(4),
        compiler_params=params(32),
        cost_estimate=cost(1.3),
        name="attend_near",
    )(block_mask, q_keep, *[near[m] for m in batches[0]])
    near_batches = [[(m, near[m]) for m in batch] for batch in batches]
    far_batches = [[(m ^ half, far[m]) for m in batch] for batch in batches]
    both = [one + two for one, two in zip(near_batches, far_batches)]
    far_mine, far_other = attend_all(blocks, q_far, both, [], 5)
    own_mine, own_other = attend_all(0, q_keep, near_batches[1:] + far_batches, own_state, 1)
    from_far = across(far_mine, half, 0)
    from_far_core = across(far_other, half, 1)
    from_core = across(own_other, 0, 1)
    lined = pl.pallas_call(
        functools.partial(line_up, half, cores),
        out_shape=[bf16(share, cores * width)] * chips,
        in_specs=in_vmem(4),
        out_specs=in_vmem(chips),
        compiler_params=params(16),
        cost_estimate=cost(0.1),
        name="line_up",
    )(own_mine, from_far_core, from_core, from_far)
    heads = pl.pallas_call(
        functools.partial(project_heads, cut),
        out_shape=[bf16(share, cores * width + head)] * peers,
        in_specs=in_vmem(peers + 2),
        out_specs=in_vmem(peers),
        compiler_params=params(32),
        cost_estimate=cost(0.3),
        name="project_heads",
    )(*lined[1:], right, core_weight)
    tails = pl.pallas_call(
        project_tails,
        out_shape=[bf16(share, columns - cut - head)] * peers,
        in_specs=in_vmem(peers + 2),
        out_specs=in_vmem(peers),
        compiler_params=params(32),
        cost_estimate=cost(0.4),
        name="project_tails",
    )(*lined[1:], right, core_weight)
    sums = [*heads, *tails]
    mine, chip_weights, *_ = lax.optimization_barrier((lined[0], chip_weights, *sums))
    own_left, own_right = pl.pallas_call(
        functools.partial(project_own, cut),
        out_shape=[f32(share, cut), f32(share, columns - cut)],
        in_specs=in_vmem(4),
        out_specs=in_vmem(2),
        compiler_params=params(32),
        cost_estimate=cost(0.1),
        name="project_own",
    )(mine, left, right, core_weight)
    firsts = [to_chip(array, step) for step, array in enumerate(heads, 1)]
    seconds = [to_chip(array, step) for step, array in enumerate(tails, 1)]
    chip_core_weights = [swap_cores(weight) for weight in chip_weights]
    gate = gate[None, :]
    anywhere = pl.BlockSpec(memory_space=pl.ANY)
    out = pl.pallas_call(
        finish_head,
        out_shape=bf16(share, columns),
        in_specs=in_vmem(3 + peers),
        out_specs=anywhere,
        scratch_shapes=[pltpu.VMEM((share, head), jnp.bfloat16), pltpu.SemaphoreType.DMA],
        compiler_params=params(16),
        cost_estimate=cost(20),
        name="finish_head",
    )(residual, gate, own_right, *firsts)
    out = pl.pallas_call(
        functools.partial(finish_left, peers, cut),
        out_shape=bf16(share, columns),
        in_specs=in_vmem(3 + 3 * peers) + [anywhere],
        out_specs=anywhere,
        scratch_shapes=[pltpu.VMEM((share, cut), jnp.bfloat16), pltpu.SemaphoreType.DMA],
        input_output_aliases={3 + 3 * peers: 0},
        compiler_params=params(32),
        cost_estimate=cost(1.5),
        name="finish_left",
    )(residual, gate, own_left, *firsts, *chip_weights, *chip_core_weights, out)
    return pl.pallas_call(
        finish_right,
        out_shape=bf16(share, columns),
        in_specs=in_vmem(3 + peers) + [pl.BlockSpec(memory_space=pl.ANY)],
        out_specs=pl.BlockSpec(memory_space=pl.ANY),
        scratch_shapes=[
            pltpu.VMEM((share, columns - cut - head), jnp.bfloat16),
            pltpu.SemaphoreType.DMA,
        ],
        input_output_aliases={3 + peers: 0},
        compiler_params=params(16),
        cost_estimate=cost(0.7),
        name="finish_right",
    )(residual, gate, own_right, *seconds, out)


def solution(mesh):
    return jax.shard_map(
        shards,
        mesh=mesh,
        in_specs=(
            P("seq", "tp"),
            P("seq", "tp"),
            P("seq", "tp"),
            P("tp", None),
            P(("seq", "tp"), None),
            P(),
            P(),
        ),
        out_specs=P(("seq", "tp"), None),
        check_vma=False,
    )
```
